256 devices in a mesh: grp: 2 (over core), gx: 16 (over y, x), gy: 8 (over z).
Axes of the slice: x: 4, y: 4, z: 8, core: 2. Of those that a mesh axis runs over, the one named last changes fastest.
Arguments:
- meso_wind: float32 [3, 64, 1024, 1024], P(None, None, ('grp', 'gx'), 'gy'), may hold values from -4 to 4
- old_boxes: float32 [512, 3, 65536], P(('grp', 'gx', 'gy')), may hold values from -5 to 5
- box_old_slot: int32 [256], replicated, may hold values from 0 to 511, as said below
- box_new_slot: int32 [256], replicated, may hold values from 0 to 511, as said below
- anchor_x: int32 [256], replicated, may hold values from 0 to 1022
- anchor_y: int32 [256], replicated, may hold values from 0 to 1022
- box_offset: int32 [256, 2], replicated, may hold values from 0 to 36
- wind_shift: int32 [256, 2], replicated, may hold values from -16 to 16
- point_xy: float32 [256, 64, 2], replicated, may hold values from 4 to 60
- point_z: float32 [256, 64], replicated, may hold values from 2 to 14
- point_coef: float32 [256, 64], replicated, may hold values from 0.5 to 4
Outputs:
- meso_next: float32 [3, 64, 1024, 1024], P(None, None, ('grp', 'gx'), 'gy')
- new_boxes: float32 [512, 3, 65536], P(('grp', 'gx', 'gy'))
The draws below stay inside these ranges and needn't reach their ends.
Inputs may be any that keep to these rules, and one draw needn't show every extreme that they name: `box_old_slot`: slot s belongs to device s // 2, devices counted in the order grp, gx, gy with grp slowest. Distinct boxes have distinct slots; a device holds 0 to 2 boxes, and some device holds 2. `box_new_slot`: slot s belongs to device s // 2, devices counted in the order grp, gx, gy with grp slowest. Distinct boxes have distinct slots; a device holds 0 to 2 boxes, and some device holds 2.
All inputs are finite; a program needn't handle non-finite values.
Results may differ from the reference program's by a relative error of at most 0.0003.
Values sent between devices are 32-bit elements; how exact they have to be, the bound alone decides.
A program may use at most 128 MiB of HBM per device.

```python
import math
import jax
import jax.numpy as jnp
import numpy as np
from jax import lax

LEVELS = 64
BOX_W = 64
BOX_Z = 16
RATIO = 100
SLOT_DEV = 2
POINTS = 64
SHIFT_MAX = 16
PATCH_Z = 5
BOXES = 256
SLOTS = 512
CELLS = 65536
GRID_X = 1024
GRID_Y = 1024
DEVICES = 256


def slot_table(key):
    device_key, order_key = jax.random.split(key)
    shuffled = jax.random.permutation(device_key, DEVICES - 2).astype(jnp.int32) + 1
    twin_count = BOXES // 4
    single_count = BOXES // 2
    twin_devices = jnp.concatenate([jnp.full((1,), DEVICES - 1, jnp.int32), shuffled[:twin_count - 1]])
    single_devices = jnp.concatenate([jnp.zeros((1,), jnp.int32), shuffled[twin_count - 1:twin_count - 1 + single_count - 1]])
    twin_slots = (twin_devices[:, None] * SLOT_DEV + jnp.arange(2, dtype=jnp.int32)[None, :]).reshape(-1)
    single_slots = single_devices * SLOT_DEV
    slot_list = jnp.concatenate([twin_slots, single_slots]).astype(jnp.int32)
    box_order = jax.random.permutation(order_key, BOXES).astype(jnp.int32)
    return jnp.zeros((BOXES,), jnp.int32).at[box_order].set(slot_list)


def draw_box_old_slot(key, part):
    key = jax.random.fold_in(key, 11)
    return slot_table(key)


def draw_box_new_slot(key, part):
    key = jax.random.fold_in(key, 23)
    return slot_table(key)


def touch_ends(values, own_key, low, largest):
    place = [jax.random.randint(jax.random.fold_in(own_key, axis), (), 0, length) for axis, length in enumerate(values.shape)]
    widest = values.shape.index(max(values.shape))
    next_to = place[:widest] + [(place[widest] + 1) % values.shape[widest]] + place[widest + 1:]
    return values.at[tuple(place)].set(low).at[tuple(next_to)].set(largest)


def shard_levels(stream_key, dims, shards, least, top_value):
    level, own = 1.0, jax.random.fold_in(stream_key, 6)
    for position, shards_of in shards:
        heights = jnp.exp(jax.random.uniform(jax.random.fold_in(own, position), (shards_of,), jnp.float32, least / len(shards), top_value / len(shards)))
        level = level * jnp.repeat(heights, dims[position] // shards_of).reshape([-1 if axis == position else 1 for axis in range(len(dims))])
    return level


def gaussian(rng, dims, scale, limit, pieces=(), kind=jnp.bfloat16):
    result = scale * jax.random.normal(rng, dims, jnp.float32)
    if pieces:
        result = result * shard_levels(rng, dims, pieces, -0.22, 0.18)
    return jnp.clip(result, -limit, limit).astype(kind)


def setup_inputs(seed: int = 0) -> dict:
    key_list = jax.random.split(jax.random.key(seed), 12)
    meso_wind = gaussian(key_list[0], (3, LEVELS, GRID_X, GRID_Y), 1.0, 4.0, ((2, 32), (3, 8)), jnp.float32)
    old_boxes = gaussian(key_list[1], (SLOTS, 3, CELLS), 1.0, 5.0, ((0, 256),), jnp.float32)
    box_old_slot = draw_box_old_slot(jax.random.fold_in(key_list[11], 71), 0)
    box_new_slot = draw_box_new_slot(jax.random.fold_in(key_list[11], 71), 0)
    anchor_x = touch_ends(jax.random.randint(key_list[4], (BOXES,), 0, GRID_X - 1), jax.random.fold_in(key_list[4], 1), 0, (GRID_X - 1) - 1).astype(jnp.int32)
    anchor_y = touch_ends(jax.random.randint(key_list[5], (BOXES,), 0, GRID_Y - 1), jax.random.fold_in(key_list[5], 1), 0, (GRID_Y - 1) - 1).astype(jnp.int32)
    box_offset = touch_ends(jax.random.randint(key_list[6], (BOXES, 2), 0, RATIO - BOX_W + 1), jax.random.fold_in(key_list[6], 1), 0, RATIO - BOX_W).astype(jnp.int32)
    wind_shift = touch_ends(jax.random.randint(key_list[7], (BOXES, 2), -SHIFT_MAX, SHIFT_MAX + 1), jax.random.fold_in(key_list[7], 1), -SHIFT_MAX, SHIFT_MAX).astype(jnp.int32)
    point_xy = jnp.clip(jax.random.uniform(key_list[8], (BOXES, POINTS, 2), jnp.float32, 4.0, 60.0), 4.0, 60.0)
    point_z = jnp.clip(jax.random.uniform(key_list[9], (BOXES, POINTS), jnp.float32, 2.0, 14.0), 2.0, 14.0)
    point_coef = jnp.clip(jnp.exp(jax.random.uniform(key_list[10], (BOXES, POINTS), jnp.float32, math.log(0.5), math.log(4.0))), 0.5, 4.0)
    return {"meso_wind": meso_wind, "old_boxes": old_boxes, "box_old_slot": box_old_slot, "box_new_slot": box_new_slot, "anchor_x": anchor_x, "anchor_y": anchor_y, "box_offset": box_offset, "wind_shift": wind_shift, "point_xy": point_xy, "point_z": point_z, "point_coef": point_coef}


TIME_STEP = 0.2
VISCOSITY = 0.1
KERNEL_WIDTH = 2.0
FORCE_GAIN = 20.0
PRECISE = lax.Precision.HIGHEST

def level_table():
    fine_index = np.arange(BOX_Z)
    height = np.maximum((fine_index - 1.5) / 4.0, 0.0)
    below_k = np.floor(height).astype(np.int32)
    fraction = (height - below_k).astype(np.float32)
    weights = np.zeros((BOX_Z, PATCH_Z), np.float32)
    weights[fine_index, below_k] += 1.0 - fraction
    weights[fine_index, below_k + 1] += fraction
    return weights

def meso_update(wind_field, framed_wind):
    stacked = jnp.pad(framed_wind, ((0, 0), (1, 1), (0, 0), (0, 0)))
    centre = wind_field
    west_cell = stacked[:, 1:-1, :-2, 1:-1]
    east_cell = stacked[:, 1:-1, 2:, 1:-1]
    south_cell = stacked[:, 1:-1, 1:-1, :-2]
    north_cell = stacked[:, 1:-1, 1:-1, 2:]
    below_cell = stacked[:, :-2, 1:-1, 1:-1]
    above_cell = stacked[:, 2:, 1:-1, 1:-1]
    speed_x = wind_field[0:1]
    speed_y = wind_field[1:2]
    speed_z = wind_field[2:3]
    advect = speed_x * jnp.where(speed_x > 0, centre - west_cell, east_cell - centre)
    advect = advect + speed_y * jnp.where(speed_y > 0, centre - south_cell, north_cell - centre)
    advect = advect + speed_z * jnp.where(speed_z > 0, centre - below_cell, above_cell - centre)
    laplace = west_cell + east_cell + south_cell + north_cell + below_cell + above_cell - 6.0 * centre
    return centre - TIME_STEP * advect + TIME_STEP * VISCOSITY * laplace

def gauss_line(distance):
    return jnp.exp(-(distance / KERNEL_WIDTH) ** 2) / (math.sqrt(math.pi) * KERNEL_WIDTH)

def prepare_box(box_rows, patches, offsets, shifts, points_xy, points_z, row_ids, level_weights):
    levels = row_ids // BOX_W
    across = row_ids % BOX_W
    columns = jnp.arange(BOX_W, dtype=jnp.int32)
    level_hot = (levels[:, None] == jnp.arange(BOX_Z, dtype=jnp.int32)[None, :]).astype(jnp.float32)
    vertical = jnp.dot(level_hot, level_weights, precision=PRECISE)
    across_f = across.astype(jnp.float32)
    columns_f = columns.astype(jnp.float32)
    levels_f = levels.astype(jnp.float32)
    right_x = (offsets[:, 0:1].astype(jnp.float32) + across_f[None, :] + 0.5) / RATIO
    right_y = (offsets[:, 1:2].astype(jnp.float32) + columns_f[None, :] + 0.5) / RATIO
    weight_x = jnp.stack([1.0 - right_x, right_x], axis=1)
    weight_y = jnp.stack([1.0 - right_y, right_y], axis=1)
    level_mix = jnp.einsum('bckxy,rk->bcxyr', patches, vertical, precision=PRECISE)
    coarse = jnp.einsum('bcxyr,bxr,byj->bcrj', level_mix, weight_x, weight_y, precision=PRECISE)
    source_i = across[None, :] + shifts[:, 0:1]
    source_j = columns[None, :] + shifts[:, 1:2]
    inside_i = (source_i >= 0) & (source_i < BOX_W)
    inside_j = (source_j >= 0) & (source_j < BOX_W)
    valid_cell = inside_i[:, :, None] & inside_j[:, None, :]
    merged = jnp.where(valid_cell[:, None], box_rows, coarse)
    kernel_x = gauss_line(across_f[None, None, :] + 0.5 - points_xy[:, :, 0:1])
    kernel_z = gauss_line(levels_f[None, None, :] + 0.5 - points_z[:, :, None])
    row_kernel = kernel_x * kernel_z
    column_kernel = gauss_line(columns_f[None, None, :] + 0.5 - points_xy[:, :, 1:2])
    return (merged, row_kernel, column_kernel)

def partial_sample(merged, row_kernel, column_kernel):
    row_sums = jnp.einsum('bcrj,bpj->bcrp', merged, column_kernel, precision=PRECISE)
    return jnp.einsum('bpr,bcrp->bcp', row_kernel, row_sums, precision=PRECISE)

def apply_force(merged, sample, coefficient, row_kernel, column_kernel):
    magnitude = jnp.sqrt(1.0 + lax.optimization_barrier(jnp.sum(sample * sample, axis=1, keepdims=True)))
    forces = -0.5 * coefficient[:, None, :] * magnitude * sample
    spread = jnp.einsum('bcp,bpr,bpj->bcrj', forces, row_kernel, column_kernel, precision=PRECISE)
    return merged + FORCE_GAIN * spread

def reference(meso_wind, old_boxes, box_old_slot, box_new_slot, anchor_x, anchor_y, box_offset, wind_shift, point_xy, point_z, point_coef):
    framed_wind = jnp.pad(meso_wind, ((0, 0), (0, 0), (1, 1), (1, 1)))
    meso_next = meso_update(meso_wind, framed_wind)
    pair_steps = jnp.arange(2, dtype=jnp.int32)
    columns_x = anchor_x[:, None] + pair_steps[None, :]
    columns_y = anchor_y[:, None] + pair_steps[None, :]
    low_levels = meso_wind[:, :PATCH_Z]
    picked = low_levels[:, :, columns_x[:, :, None], columns_y[:, None, :]]
    patches = jnp.transpose(picked, (2, 0, 1, 3, 4))
    level_weights = jnp.asarray(level_table())
    row_ids = jnp.arange(BOX_Z * BOX_W, dtype=jnp.int32)

    def one_box(inputs):
        old_slot, patch_one, offset_one, shift_one, xy_one, height_one, coef_one = inputs
        old_box = lax.dynamic_index_in_dim(old_boxes, old_slot.astype(jnp.int32), 0, keepdims=False)
        box_grid = old_box.reshape(3, BOX_Z, BOX_W, BOX_W)
        framed_box = jnp.pad(box_grid, ((0, 0), (0, 0), (SHIFT_MAX, SHIFT_MAX), (SHIFT_MAX, SHIFT_MAX)))
        start_i = (SHIFT_MAX + shift_one[0]).astype(jnp.int32)
        start_j = (SHIFT_MAX + shift_one[1]).astype(jnp.int32)
        zero_index = jnp.zeros((), jnp.int32)
        shifted = lax.dynamic_slice(framed_box, (zero_index, zero_index, start_i, start_j), (3, BOX_Z, BOX_W, BOX_W))
        box_rows = shifted.reshape(1, 3, BOX_Z * BOX_W, BOX_W)
        merged, row_kernel, column_kernel = prepare_box(box_rows, patch_one[None], offset_one[None], shift_one[None], xy_one[None], height_one[None], row_ids, level_weights)
        sample = partial_sample(merged, row_kernel, column_kernel)
        finished = apply_force(merged, sample, coef_one[None], row_kernel, column_kernel)
        return finished.reshape(3, CELLS)
    results = lax.map(one_box, (box_old_slot, patches, box_offset, wind_shift, point_xy, point_z, point_coef))
    new_boxes = jnp.zeros((SLOTS, 3, CELLS), jnp.float32).at[box_new_slot].set(results)
    return (meso_next, new_boxes)
```

```python
import functools
import math

import jax
import jax.numpy as jnp
import numpy as np
from jax import lax
from jax.experimental import pallas as pl
from jax.experimental.pallas import tpu as pltpu
from jax.sharding import PartitionSpec as P

MESH = pl.DeviceIdType.MESH
F32 = jnp.float32
I32 = jnp.int32
PRECISE = lax.Precision.HIGHEST
BOX_Z = 16
PATCH_Z = 5
RATIO = 100
TIME_STEP = 0.2
VISCOSITY = 0.1
KERNEL_WIDTH = 2.0
FORCE_GAIN = 20.0
NX, NZ = 32, 8
PLACES = 64
USUAL = 12
ROWS = 512
SHARE = ROWS // NX
MARGIN = 16


def level_table():
    table = []
    for level in range(BOX_Z):
        height = max((level - 1.5) / 4.0, 0.0)
        below = int(math.floor(height))
        table.append((below, height - below))
    return table


def position():
    grp, gx, z = lax.axis_index("grp"), lax.axis_index("gx"), lax.axis_index("gy")
    return grp * 16 + gx, z


def device(p, z):
    return (p // 16, lax.rem(p, 16), z)


def iota(shape, dim):
    return lax.broadcasted_iota(I32, shape, dim)


def dot_nt(a, b):
    return lax.dot_general(a, b, (((1,), (1,)), ((), ())), precision=PRECISE, preferred_element_type=F32)


def tables_kernel(old_ref, new_ref, send_ref, usual_ref, full_ref, most_ref):
    z = lax.axis_index("gy")
    boxes = old_ref.shape[1]
    old_row, new_row = old_ref[...], new_ref[...]
    across, down = iota((boxes, boxes), 1), iota((boxes, boxes), 0)
    same = across == down

    def column(row):
        return jnp.sum(jnp.where(same, row.astype(F32), 0.0), axis=1, keepdims=True).astype(I32)

    old_col, new_col = column(old_row), column(new_row)
    z_old, z_new = (old_col >> 1) & 7, (new_col >> 1) & 7
    pair_col = z_old * NZ + z_new
    pair_row = ((old_row >> 1) & 7) * NZ + ((new_row >> 1) & 7)
    before = (pair_row == pair_col) & (across < down)
    rank_f = jnp.sum(jnp.where(before, 1.0, 0.0), axis=1, keepdims=True)
    rank = rank_f.astype(I32)
    old_local = (old_col >> 4) * 2 + (old_col & 1)
    new_local = (new_col >> 4) * 2 + (new_col & 1)
    sends = jnp.where(z_old == z, z_new * PLACES + rank, -1)
    takes = jnp.where(z_new == z, new_local, -1)
    send_hot = iota((boxes, NZ * PLACES), 1) == sends
    take_hot = iota((boxes, 128), 1) == takes
    send_ref[...] = jnp.sum(
        jnp.where(send_hot, old_local.astype(F32), 0.0), axis=0, keepdims=True
    ).astype(I32)
    for ref, places in ((usual_ref, USUAL), (full_ref, PLACES)):
        at = (z_old * places + rank).astype(F32)
        ref[...] = jnp.sum(jnp.where(take_hot, at, 0.0), axis=0, keepdims=True).astype(I32)
    most = jnp.max(rank_f, axis=0, keepdims=True).astype(I32)
    most_ref[...] = jnp.broadcast_to(most, (1, 128))


def meso_levels(m, halo_y, mout, p, z, first, last):
    lane = iota((32, 128), 1)
    has_south, has_north = z > 0, z < NZ - 1

    def level(k, _):
        winds = [m[c, k + 1, 8:40, :] for c in range(3)]
        u, v, w = winds
        for c in range(3):
            q = winds[c]
            west, east = m[c, k + 1, 7:39, :], m[c, k + 1, 9:41, :]
            below, above = m[c, k, 8:40, :], m[c, k + 2, 8:40, :]
            tile = 128 if c == 2 else 0
            at = k + (64 if c == 1 else 0)
            south_edge = pltpu.roll(halo_y[0, :, tile : tile + 128], 128 - at, 1)
            north_edge = pltpu.roll(halo_y[1, :, tile : tile + 128], 127 - at, 1)
            south_edge = jnp.where(has_south, south_edge, 0.0)
            north_edge = jnp.where(has_north, north_edge, 0.0)
            south = jnp.where(lane == 0, south_edge, pltpu.roll(q, 1, 1))
            north = jnp.where(lane == 127, north_edge, pltpu.roll(q, 127, 1))
            advect = u * jnp.where(u > 0, q - west, east - q)
            advect = advect + v * jnp.where(v > 0, q - south, north - q)
            advect = advect + w * jnp.where(w > 0, q - below, above - q)
            laplace = west + east + south + north + below + above - 6.0 * q
            mout[c, k] = q - TIME_STEP * advect + TIME_STEP * VISCOSITY * laplace
        return 0

    lax.fori_loop(first, last, level, 0)


def exchange_kernel(
    places,
    old,
    meso,
    send_tab,
    take_tab,
    new_ref,
    ax_ref,
    ay_ref,
    offset_ref,
    shift_ref,
    pxy_ref,
    pz_ref,
    pc_ref,
    boxes_out,
    meso_out,
    patch_out,
    points_out,
    ints_out,
    r,
    rd,
    zs,
    zr,
    ps,
    m,
    mout,
    hxs,
    hxr,
    hys,
    hyr,
    bt,
    ts,
    tr,
    tz,
    tzr,
    send_sem,
    a_sem,
    z_sem,
    p_sem,
    t_sem,
    tz_sem,
    h_sem,
    local_sem,
):
    p, z = position()
    barrier = pltpu.get_barrier_semaphore()

    def greet_z(d, _):
        pl.semaphore_signal(
            barrier, inc=1, device_id=device(p, lax.rem(z + d, NZ)), device_id_type=MESH
        )
        return 0

    def greet_plane(d, _):
        pl.semaphore_signal(
            barrier, inc=1, device_id=device(lax.rem(p + d, NX), z), device_id_type=MESH
        )
        return 0

    lax.fori_loop(1, NZ, greet_z, 0)
    lax.fori_loop(1, NX, greet_plane, 0)

    load = pltpu.make_async_copy(meso, m.at[:, pl.ds(1, 64), pl.ds(8, 32), :], local_sem.at[3])
    load.start()
    zero_level = jnp.zeros((48, 128), F32)
    for c in range(3):
        m[c, 0] = zero_level
        m[c, 65] = zero_level
    load.wait()

    for c in range(3):
        hxs[0, c * 64 : (c + 1) * 64, :] = m[c, 1:65, 39, :]
        hxs[1, c * 64 : (c + 1) * 64, :] = m[c, 1:65, 8, :]
    lane = iota((32, 128), 1)

    def pack(k, held):
        top0, top1, low0, low1 = held
        for c in range(3):
            q = m[c, k + 1, 8:40, :]
            at = k + (64 if c == 1 else 0)
            here = lane == at
            top = pltpu.roll(q, at + 1, 1)
            low = pltpu.roll(q, at, 1)
            if c < 2:
                top0, low0 = jnp.where(here, top, top0), jnp.where(here, low, low0)
            else:
                top1, low1 = jnp.where(here, top, top1), jnp.where(here, low, low1)
        return top0, top1, low0, low1

    blank = jnp.zeros((32, 128), F32)
    top0, top1, low0, low1 = lax.fori_loop(0, 64, pack, (blank, blank, blank, blank))
    hys[0, :, 0:128] = top0
    hys[0, :, 128:256] = top1
    hys[1, :, 0:128] = low0
    hys[1, :, 128:256] = low1

    pl.semaphore_wait(barrier, NX + NZ - 2)

    def start_plane(src_of, dst_of, recv, sent):
        def one(d, _):
            t = lax.rem(p + d, NX)
            pltpu.make_async_remote_copy(
                src_of(t), dst_of(), sent, recv, device_id=device(t, z), device_id_type=MESH
            ).start()
            return 0

        lax.fori_loop(1, NX, one, 0)
        pltpu.make_async_copy(src_of(p), dst_of(), recv).start()

    def start_z(src_of, dst_of, recv, sent):
        def one(d, _):
            t = lax.rem(z + d, NZ)
            pltpu.make_async_remote_copy(
                src_of(t), dst_of(), sent, recv, device_id=device(p, t), device_id_type=MESH
            ).start()
            return 0

        lax.fori_loop(1, NZ, one, 0)
        pltpu.make_async_copy(src_of(z), dst_of(), recv).start()

    def wait_all(ref, sem):
        pltpu.make_async_copy(ref, ref, sem).wait()

    def spread(c):
        start_plane(
            lambda t: old.at[c, pl.ds(pl.multiple_of(t * 32, 32), 32), :],
            lambda: r.at[c, pl.ds(pl.multiple_of(p * 32, 32), 32), :],
            a_sem.at[c],
            send_sem.at[c],
        )

    spread(0)
    halos = [
        (hxs.at[0], hxr.at[0], device(lax.rem(p + 1, NX), z)),
        (hxs.at[1], hxr.at[1], device(lax.rem(p + NX - 1, NX), z)),
        (hys.at[0], hyr.at[0], device(p, lax.rem(z + 1, NZ))),
        (hys.at[1], hyr.at[1], device(p, lax.rem(z + NZ - 1, NZ))),
    ]
    for at, (src, dst, target) in enumerate(halos):
        pltpu.make_async_remote_copy(
            src, dst, send_sem.at[9 + at], h_sem.at[at], device_id=target, device_id_type=MESH
        ).start()
    spread(1)
    spread(2)

    bt[...] = jnp.zeros_like(bt)
    for c in range(3):
        for k in range(PATCH_Z):
            bt[pl.ds(c * PATCH_Z + k, 32, stride=16), :] = m[c, k + 1, 8:40, :]
    columns = bt[...]
    new_row = new_ref[...]
    local_x = ax_ref[...] - p * 32
    local_y = ay_ref[...] - z * 128
    boxes = new_row.shape[1]
    depth = iota((128, boxes), 0)
    corners = [None] * 4
    for f in range(2):
        hot = jnp.where(depth == local_y + f, 1.0, 0.0)
        picked = jnp.dot(columns, hot, precision=PRECISE, preferred_element_type=F32)
        for e in range(2):
            total = jnp.zeros((16, boxes), F32)
            for x in range(32):
                here = jnp.where(local_x + e == x, 1.0, 0.0)
                total = total + picked[x * 16 : (x + 1) * 16] * here
            corners[e * 2 + f] = total
    terms = jnp.concatenate(corners, axis=0)
    odd = (new_row & 1).astype(F32)
    terms = jnp.concatenate([terms * (1.0 - odd), terms * odd], axis=0)
    owner = jnp.where((new_row >> 1) == iota((boxes, boxes), 0), 1.0, 0.0)
    ts[...] = dot_nt(owner, terms).reshape(NX, NZ, 128)
    start_plane(lambda t: ts.at[t], lambda: tr.at[p], t_sem, send_sem.at[13])

    def to_z(c):
        wait_all(r.at[c], a_sem.at[c])

        def part_slots(t, _):
            for s in range(2):
                for half in range(2):
                    rows = pl.ds(pl.multiple_of(t * 32, 32) + half * 16 + s, 8, stride=2)
                    rd[c][t * 2 + s, half * 8 : half * 8 + 8, :] = r[c, rows, :]
            return 0

        lax.fori_loop(0, NX, part_slots, 0, unroll=2)

        def one(e, _):
            zt, q = e // places, lax.rem(e, places)
            place = send_tab[0, zt * PLACES + q]
            zs[c][e] = rd[c][place]
            return 0

        lax.fori_loop(0, NZ * places, one, 0, unroll=4)
        start_z(
            lambda t: zs[c].at[pl.ds(t * places, places)],
            lambda: zr[c].at[pl.ds(z * places, places)],
            z_sem.at[c],
            send_sem.at[3 + c],
        )

    def to_owner(c):
        wait_all(zr[c], z_sem.at[c])

        def one(t, _):
            for s in range(2):
                ps[c][t, s] = zr[c][take_tab[0, t * 2 + s]]
            return 0

        lax.fori_loop(0, NX, one, 0, unroll=2)
        start_plane(
            lambda t: ps[c].at[t],
            lambda: boxes_out.at[c, :, pl.ds(pl.multiple_of(p * SHARE, SHARE), SHARE), :],
            p_sem.at[c],
            send_sem.at[6 + c],
        )

    to_z(0)
    for at, (_, dst, _) in enumerate(halos):
        wait_all(dst, h_sem.at[at])
    for c in range(3):
        block = slice(c * 64, (c + 1) * 64)
        m[c, 1:65, 7, :] = jnp.where(p > 0, hxr[0, block, :], 0.0)
        m[c, 1:65, 40, :] = jnp.where(p < NX - 1, hxr[1, block, :], 0.0)
    stores = []
    for part, (first, last) in enumerate(((0, 22), (22, 44), (44, 64))):
        if part:
            to_z(part)
        meso_levels(m, hyr, mout, p, z, first, last)
        span = pl.ds(first, last - first)
        stores.append(pltpu.make_async_copy(mout.at[:, span], meso_out.at[:, span], local_sem.at[part]))
        stores[-1].start()

    wait_all(tr, t_sem)
    summed = jnp.sum(tr[...], axis=0)
    for t in range(NZ):
        tz[t] = summed[t : t + 1]
    start_z(lambda t: tz.at[t], lambda: tzr.at[z], tz_sem, send_sem.at[14])

    mine = (p * NZ + z) * 2
    hot = jnp.where(new_row == mine + iota((8, boxes), 0), 1.0, 0.0)
    px, py = pxy_ref[:, 0, :], pxy_ref[:, 1, :]
    pz, pc = pz_ref[...], pc_ref[...]
    points_out[...] = dot_nt(hot, jnp.concatenate([px, px, py, py, pz, pz, pc, pc], axis=0))
    fields = jnp.concatenate(
        [
            offset_ref[...].astype(F32),
            shift_ref[...].astype(F32),
            jnp.ones((1, boxes), F32),
            jnp.zeros((123, boxes), F32),
        ],
        axis=0,
    )
    ints_out[...] = jnp.round(dot_nt(hot, fields)).astype(I32)

    for c in range(3):
        to_owner(c)
    wait_all(tzr, tz_sem)
    patch_out[...] = jnp.sum(tzr[...], axis=0)

    for store in stores:
        store.wait()
    for c in range(3):
        wait_all(boxes_out.at[c], p_sem.at[c])

    def sent(ref, sem):
        pltpu.make_async_remote_copy(
            ref, ref, sem, h_sem.at[0], device_id=device(p, z), device_id_type=MESH
        ).wait_send()

    for c in range(3):
        sent(r.at[c, pl.ds(0, 31 * 32), :], send_sem.at[c])
        sent(zs[c].at[pl.ds(0, (NZ - 1) * places)], send_sem.at[3 + c])
        sent(ps[c].at[pl.ds(0, NX - 1)], send_sem.at[6 + c])
    for at in range(4):
        sent(halos[at][0], send_sem.at[9 + at])
    sent(ts.at[pl.ds(0, NX - 1)], send_sem.at[13])
    sent(tz.at[pl.ds(0, NZ - 1)], send_sem.at[14])


def split_pair(a):
    high = a.astype(jnp.bfloat16)
    return high, (a - high.astype(F32)).astype(jnp.bfloat16)


def gauss_line(distance):
    return jnp.exp(-((distance / KERNEL_WIDTH) ** 2)) / (math.sqrt(math.pi) * KERNEL_WIDTH)


def box_kernel(boxes, meso, patch, points, ints, out, meso_out, held, merged, load_sem, meso_sem):
    through = pltpu.make_async_copy(meso, meso_out, meso_sem)
    through.start()
    loads = []
    for s in range(2):
        for c in range(3):
            loads.append(
                pltpu.make_async_copy(
                    boxes.at[c, s], held.at[s, c, pl.ds(MARGIN, ROWS), :], load_sem.at[s * 3 + c]
                )
            )
            loads[-1].start()
    lane, h = iota((32, 128), 1), iota((32, 128), 0)
    i, j = 2 * h + (lane >> 6), lane & 63
    tall, wide = iota((128, 128), 0), iota((128, 128), 1)
    table = level_table()
    for s in range(2):
        ox, oy, sx, sy, occupied = [ints[s, at] for at in range(5)]
        flat = sx * 64 + sy
        rows, turn = flat >> 7, flat & 127
        valid = (i + sx >= 0) & (i + sx < 64) & (j + sy >= 0) & (j + sy < 64)
        right_x = ((ox + i).astype(F32) + 0.5) / RATIO
        right_y = ((oy + j).astype(F32) + 0.5) / RATIO
        left_x, left_y = 1.0 - right_x, 1.0 - right_y
        weights = [left_x * left_y, left_x * right_y, right_x * left_y, right_x * right_y]
        x_row = points[s : s + 1, 0:128]
        y_row = points[s : s + 1, 128:256]
        z_row = points[s : s + 1, 256:384]
        coef = points[s : s + 1, 384:512]
        kx = gauss_line((2 * iota((32, 128), 0) + (lane >> 6)).astype(F32) + 0.5 - x_row)
        kz = gauss_line(iota((BOX_Z, 128), 0).astype(F32) + 0.5 - z_row)
        ky = gauss_line((tall & 63).astype(F32) + 0.5 - y_row)
        ky = jnp.where((tall >> 6) == (wide >> 6), ky, 0.0)
        ky_high, ky_low = split_pair(ky)
        twice = jnp.concatenate([ky_high, ky_low], axis=1)
        sample_w = jnp.concatenate([twice, twice], axis=0)
        spread_w = jnp.concatenate(
            [jnp.concatenate([ky_high, ky_high], axis=1), jnp.concatenate([ky_low, ky_low], axis=1)], axis=0
        )
        samples = []
        for c in range(3):
            loads[s * 3 + c].wait()
            planes = []
            for k in range(PATCH_Z):
                plane = weights[0] * patch[0, s * 64 + c * PATCH_Z + k]
                for at in range(1, 4):
                    plane = plane + weights[at] * patch[0, s * 64 + at * 16 + c * PATCH_Z + k]
                planes.append(plane)
            for level in range(BOX_Z):
                below, part = table[level]
                fill = planes[below]
                if part:
                    fill = (1.0 - part) * fill + part * planes[below + 1]
                start = MARGIN + level * 32 + rows
                first = held[s, c, pl.ds(start, 32), :]
                second = held[s, c, pl.ds(start + 1, 32), :]
                moved = pltpu.roll(jnp.where(lane >= turn, first, second), 128 - turn, 1)
                merged[s, c, level * 32 : (level + 1) * 32, :] = jnp.where(valid, moved, fill)
            block = merged[s, c]
            high, low = split_pair(block)
            both = jnp.dot(
                jnp.concatenate([high, low], axis=1), sample_w, preferred_element_type=F32
            )
            sums = (both[:, :128] + both[:, 128:]).reshape(BOX_Z, 32, 128) * kx[None]
            per_level = jnp.sum(sums, axis=1) * kz
            half = jnp.sum(per_level, axis=0, keepdims=True)
            samples.append(half + pltpu.roll(half, 64, 1))
        magnitude = jnp.sqrt(1.0 + (samples[0] ** 2 + samples[1] ** 2 + samples[2] ** 2))
        shape = (kz[:, None, :] * kx[None]).reshape(ROWS, 128)
        for c in range(3):
            force = FORCE_GAIN * (-0.5 * coef * magnitude * samples[c])
            high, low = split_pair(shape * force)
            both = lax.dot_general(
                jnp.concatenate([high, low], axis=1),
                spread_w,
                (((1,), (1,)), ((), ())),
                preferred_element_type=F32,
            )
            finished = merged[s, c] + (both[:, :128] + both[:, 128:])
            out[c, pl.ds(s, ROWS, stride=2), :] = jnp.where(occupied > 0, finished, 0.0)
    through.wait()


def vmem():
    return pl.BlockSpec(memory_space=pltpu.VMEM)


def smem():
    return pl.BlockSpec(memory_space=pltpu.SMEM)


def anywhere():
    return pl.BlockSpec(memory_space=pl.ANY)


def exchange(places, collective_id, operands):
    shape = jax.ShapeDtypeStruct
    dma = pltpu.SemaphoreType.DMA
    return pl.pallas_call(
        functools.partial(exchange_kernel, places),
        out_shape=(
            shape((3, 2, ROWS, 128), F32),
            shape((3, 64, 32, 128), F32),
            shape((1, 128), F32),
            shape((8, 512), F32),
            shape((8, 128), I32),
        ),
        in_specs=[anywhere(), anywhere(), smem(), smem()] + [vmem()] * 8,
        out_specs=(anywhere(), anywhere(), vmem(), vmem(), vmem()),
        scratch_shapes=[
            pltpu.VMEM((3, 2 * ROWS, 128), F32),
            (pltpu.VMEM((2 * NX, SHARE, 128), F32),) * 3,
            (pltpu.VMEM((NZ * places, SHARE, 128), F32),) * 3,
            (pltpu.VMEM((NZ * places, SHARE, 128), F32),) * 3,
            (pltpu.VMEM((NX, 2, SHARE, 128), F32),) * 3,
            pltpu.VMEM((3, 66, 48, 128), F32),
            pltpu.VMEM((3, 64, 32, 128), F32),
            pltpu.VMEM((2, 192, 128), F32),
            pltpu.VMEM((2, 192, 128), F32),
            pltpu.VMEM((2, 32, 256), F32),
            pltpu.VMEM((2, 32, 256), F32),
            pltpu.VMEM((512, 128), F32),
            pltpu.VMEM((NX, NZ, 128), F32),
            pltpu.VMEM((NX, NZ, 128), F32),
            pltpu.VMEM((NZ, 1, 128), F32),
            pltpu.VMEM((NZ, 1, 128), F32),
            dma((15,)),
            dma((3,)),
            dma((3,)),
            dma((3,)),
            dma,
            dma,
            dma((4,)),
            dma((4,)),
        ],
        compiler_params=pltpu.CompilerParams(
            collective_id=collective_id, has_side_effects=True, vmem_limit_bytes=56 << 20
        ),
        name="exchange",
    )(*operands)


def local(
    meso_wind,
    old_boxes,
    box_old_slot,
    box_new_slot,
    anchor_x,
    anchor_y,
    box_offset,
    wind_shift,
    point_xy,
    point_z,
    point_coef,
):
    shape = jax.ShapeDtypeStruct
    old_row, new_row = box_old_slot.reshape(1, -1), box_new_slot.reshape(1, -1)
    send_tab, take_usual, take_full, most = pl.pallas_call(
        tables_kernel,
        out_shape=(shape((1, NZ * PLACES), I32),) + (shape((1, 128), I32),) * 3,
        in_specs=[vmem(), vmem()],
        out_specs=(vmem(),) * 4,
        name="tables",
    )(old_row, new_row)
    old = jnp.transpose(old_boxes.reshape(2, 3, ROWS, 128), (1, 2, 0, 3)).reshape(3, 2 * ROWS, 128)
    operands = (
        old,
        meso_wind,
        send_tab,
        take_usual,
        take_full,
        new_row,
        anchor_x.reshape(1, -1),
        anchor_y.reshape(1, -1),
        box_offset.T,
        wind_shift.T,
        jnp.transpose(point_xy, (1, 2, 0)),
        point_z.T,
        point_coef.T,
    )
    boxes, meso_next, patch, points, ints = lax.cond(
        most[0, 0] < USUAL,
        lambda given: exchange(USUAL, 1, given[:4] + given[5:]),
        lambda given: exchange(PLACES, 2, given[:3] + given[4:]),
        operands,
    )
    new_boxes, meso_next = pl.pallas_call(
        box_kernel,
        out_shape=(shape((3, 2 * ROWS, 128), F32), shape((3, 64, 32, 128), F32)),
        in_specs=[anywhere(), anywhere(), smem(), vmem(), smem()],
        out_specs=(vmem(), anywhere()),
        scratch_shapes=[
            pltpu.VMEM((2, 3, ROWS + 2 * MARGIN, 128), F32),
            pltpu.VMEM((2, 3, ROWS, 128), F32),
            pltpu.SemaphoreType.DMA((6,)),
            pltpu.SemaphoreType.DMA,
        ],
        compiler_params=pltpu.CompilerParams(vmem_limit_bytes=40 << 20),
        name="boxes",
    )(boxes, meso_next, patch, points, ints)
    new_boxes = jnp.transpose(new_boxes.reshape(3, ROWS, 2, 128), (2, 0, 1, 3)).reshape(2, 3, ROWS * 128)
    return (meso_next, new_boxes)


def solution(mesh):
    whole = P(("grp", "gx", "gy"), None, None)
    grid = P(None, None, ("grp", "gx"), "gy")
    return jax.shard_map(
        local,
        mesh=mesh,
        in_specs=(grid, whole) + (P(),) * 9,
        out_specs=(grid, whole),
        check_vma=False,
    )
```

```python
import functools
import math

import jax
import jax.numpy as jnp
import numpy as np
from jax import lax
from jax.experimental import pallas as pl
from jax.experimental.pallas import tpu as pltpu
from jax.sharding import PartitionSpec as P

MESH = pl.DeviceIdType.MESH
F32 = jnp.float32
I32 = jnp.int32
PRECISE = lax.Precision.HIGHEST
BOX_Z = 16
PATCH_Z = 5
RATIO = 100
TIME_STEP = 0.2
VISCOSITY = 0.1
KERNEL_WIDTH = 2.0
FORCE_GAIN = 20.0
NX, NZ = 32, 8
PLACES = 64
SIZES = (8, 9, 10, 12, PLACES)
ROWS = 512
CHUNKS = 6
HALF = ROWS // 2
SHARE = HALF // NX
MARGIN = 16


def level_table():
    table = []
    for level in range(BOX_Z):
        height = max((level - 1.5) / 4.0, 0.0)
        below = int(math.floor(height))
        table.append((below, height - below))
    return table


def position():
    grp, gx, z = lax.axis_index("grp"), lax.axis_index("gx"), lax.axis_index("gy")
    return grp * 16 + gx, z


def device(p, z):
    return (p // 16, lax.rem(p, 16), z)


def iota(shape, dim):
    return lax.broadcasted_iota(I32, shape, dim)


def dot_nt(a, b):
    return lax.dot_general(a, b, (((1,), (1,)), ((), ())), precision=PRECISE, preferred_element_type=F32)


def tables_kernel(old_ref, new_ref, send_ref, take_ref, choice_ref):
    z = lax.axis_index("gy")
    boxes = old_ref.shape[1]
    old_row, new_row = old_ref[...], new_ref[...]
    across, down = iota((boxes, boxes), 1), iota((boxes, boxes), 0)
    same = across == down

    def column(row):
        return jnp.sum(jnp.where(same, row.astype(F32), 0.0), axis=1, keepdims=True).astype(I32)

    old_col, new_col = column(old_row), column(new_row)
    z_old, z_new = (old_col >> 1) & 7, (new_col >> 1) & 7
    pair_col = z_old * NZ + z_new
    pair_row = ((old_row >> 1) & 7) * NZ + ((new_row >> 1) & 7)
    before = (pair_row == pair_col) & (across < down)
    rank_f = jnp.sum(jnp.where(before, 1.0, 0.0), axis=1, keepdims=True)
    rank = rank_f.astype(I32)
    old_local = (old_col >> 4) * 2 + (old_col & 1)
    new_local = (new_col >> 4) * 2 + (new_col & 1)
    sends = jnp.where(z_old == z, z_new * PLACES + rank, -1)
    takes = jnp.where(z_new == z, new_local, -1)
    send_hot = iota((boxes, NZ * PLACES), 1) == sends
    take_hot = iota((boxes, 128), 1) == takes
    send_ref[...] = jnp.sum(
        jnp.where(send_hot, old_local.astype(F32), 0.0), axis=0, keepdims=True
    ).astype(I32)
    most = jnp.max(rank_f, axis=0, keepdims=True)
    limit = jnp.full((1, 1), SIZES[0], F32)
    choice = jnp.zeros((1, 1), F32)
    for at, size in enumerate(SIZES[1:]):
        full = most >= SIZES[at]
        limit, choice = jnp.where(full, float(size), limit), jnp.where(full, at + 1.0, choice)
    place = z_old.astype(F32) * limit + rank_f
    take_ref[...] = jnp.sum(jnp.where(take_hot, place, 0.0), axis=0, keepdims=True).astype(I32)
    choice_ref[...] = jnp.broadcast_to(choice, (1, 128)).astype(I32)


def meso_levels(m, halo_y, mout, p, z, first, last):
    lane = iota((32, 128), 1)
    has_south, has_north = z > 0, z < NZ - 1

    def level(k, _):
        winds = [m[c, k + 1, 8:40, :] for c in range(3)]
        u, v, w = winds
        for c in range(3):
            q = winds[c]
            west, east = m[c, k + 1, 7:39, :], m[c, k + 1, 9:41, :]
            below, above = m[c, k, 8:40, :], m[c, k + 2, 8:40, :]
            tile = 128 if c == 2 else 0
            at = k + (64 if c == 1 else 0)
            south_edge = pltpu.roll(halo_y[0, :, tile : tile + 128], 128 - at, 1)
            north_edge = pltpu.roll(halo_y[1, :, tile : tile + 128], 127 - at, 1)
            south_edge = jnp.where(has_south, south_edge, 0.0)
            north_edge = jnp.where(has_north, north_edge, 0.0)
            south = jnp.where(lane == 0, south_edge, pltpu.roll(q, 1, 1))
            north = jnp.where(lane == 127, north_edge, pltpu.roll(q, 127, 1))
            advect = u * jnp.where(u > 0, q - west, east - q)
            advect = advect + v * jnp.where(v > 0, q - south, north - q)
            advect = advect + w * jnp.where(w > 0, q - below, above - q)
            laplace = west + east + south + north + below + above - 6.0 * q
            mout[c, k] = q - TIME_STEP * advect + TIME_STEP * VISCOSITY * laplace
        return 0

    lax.fori_loop(first, last, level, 0)


def exchange_kernel(
    places,
    old,
    meso,
    send_tab,
    take_tab,
    new_ref,
    ax_ref,
    ay_ref,
    offset_ref,
    shift_ref,
    pxy_ref,
    pz_ref,
    pc_ref,
    boxes_out,
    meso_out,
    patch_out,
    points_out,
    ints_out,
    r,
    rd,
    zs,
    zr,
    ps,
    m,
    mout,
    hxs,
    hxr,
    hys,
    hyr,
    bt,
    ts,
    tr,
    tz,
    tzr,
    send_sem,
    a_sem,
    z_sem,
    p_sem,
    t_sem,
    tz_sem,
    h_sem,
    local_sem,
):
    p, z = position()
    barrier = pltpu.get_barrier_semaphore()

    def greet_z(d, _):
        pl.semaphore_signal(
            barrier, inc=1, device_id=device(p, lax.rem(z + d, NZ)), device_id_type=MESH
        )
        return 0

    def greet_plane(d, _):
        pl.semaphore_signal(
            barrier, inc=1, device_id=device(lax.rem(p + d, NX), z), device_id_type=MESH
        )
        return 0

    lax.fori_loop(1, NZ, greet_z, 0)
    lax.fori_loop(1, NX, greet_plane, 0)

    load = pltpu.make_async_copy(meso, m.at[:, pl.ds(1, 64), pl.ds(8, 32), :], local_sem.at[4])
    load.start()
    zero_level = jnp.zeros((48, 128), F32)
    for c in range(3):
        m[c, 0] = zero_level
        m[c, 65] = zero_level
    load.wait()

    for c in range(3):
        hxs[0, c * 64 : (c + 1) * 64, :] = m[c, 1:65, 39, :]
        hxs[1, c * 64 : (c + 1) * 64, :] = m[c, 1:65, 8, :]
    lane = iota((32, 128), 1)

    def pack(k, held):
        top0, top1, low0, low1 = held
        for c in range(3):
            q = m[c, k + 1, 8:40, :]
            at = k + (64 if c == 1 else 0)
            here = lane == at
            top = pltpu.roll(q, at + 1, 1)
            low = pltpu.roll(q, at, 1)
            if c < 2:
                top0, low0 = jnp.where(here, top, top0), jnp.where(here, low, low0)
            else:
                top1, low1 = jnp.where(here, top, top1), jnp.where(here, low, low1)
        return top0, top1, low0, low1

    blank = jnp.zeros((32, 128), F32)
    top0, top1, low0, low1 = lax.fori_loop(0, 64, pack, (blank, blank, blank, blank))
    hys[0, :, 0:128] = top0
    hys[0, :, 128:256] = top1
    hys[1, :, 0:128] = low0
    hys[1, :, 128:256] = low1

    pl.semaphore_wait(barrier, NX + NZ - 2)

    def start_plane(src_of, dst_of, recv, sent):
        def one(d, _):
            t = lax.rem(p + d, NX)
            pltpu.make_async_remote_copy(
                src_of(t), dst_of(), sent, recv, device_id=device(t, z), device_id_type=MESH
            ).start()
            return 0

        lax.fori_loop(1, NX, one, 0)
        pltpu.make_async_copy(src_of(p), dst_of(), recv).start()

    def start_z(src_of, dst_of, recv, sent):
        def one(d, _):
            t = lax.rem(z + d, NZ)
            pltpu.make_async_remote_copy(
                src_of(t), dst_of(), sent, recv, device_id=device(p, t), device_id_type=MESH
            ).start()
            return 0

        lax.fori_loop(1, NZ, one, 0)
        pltpu.make_async_copy(src_of(z), dst_of(), recv).start()

    def wait_all(ref, sem):
        pltpu.make_async_copy(ref, ref, sem).wait()

    def spread(n):
        c, half = n // 2, n % 2
        start_plane(
            lambda t: old.at[c, pl.ds(pl.multiple_of(half * 2 * HALF + t * 16, 16), 16), :],
            lambda: r[n].at[pl.ds(pl.multiple_of(p * 16, 16), 16), :],
            a_sem.at[n],
            send_sem.at[n],
        )

    spread(0)
    halos = [
        (hxs.at[0], hxr.at[0], device(lax.rem(p + 1, NX), z)),
        (hxs.at[1], hxr.at[1], device(lax.rem(p + NX - 1, NX), z)),
        (hys.at[0], hyr.at[0], device(p, lax.rem(z + 1, NZ))),
        (hys.at[1], hyr.at[1], device(p, lax.rem(z + NZ - 1, NZ))),
    ]
    for at, (src, dst, target) in enumerate(halos):
        pltpu.make_async_remote_copy(
            src, dst, send_sem.at[3 * CHUNKS + at], h_sem.at[at], device_id=target, device_id_type=MESH
        ).start()
    for n in range(1, CHUNKS):
        spread(n)

    def to_z(n):
        wait_all(r[n], a_sem.at[n])

        def part_slots(t, _):
            for s in range(2):
                rd[n][t * 2 + s] = r[n][pl.ds(pl.multiple_of(t * 16, 16) + s, 8, stride=2), :]
            return 0

        lax.fori_loop(0, NX, part_slots, 0, unroll=4)

        def one(e, _):
            zt, q = e // places, lax.rem(e, places)
            zs[n][e] = rd[n][send_tab[0, zt * PLACES + q]]
            return 0

        lax.fori_loop(0, NZ * places, one, 0, unroll=4)
        start_z(
            lambda t: zs[n].at[pl.ds(t * places, places)],
            lambda: zr[n].at[pl.ds(z * places, places)],
            z_sem.at[n],
            send_sem.at[CHUNKS + n],
        )

    def to_owner(n):
        c, half = n // 2, n % 2
        wait_all(zr[n], z_sem.at[n])

        def one(t, _):
            for s in range(2):
                ps[n][t, s] = zr[n][take_tab[0, t * 2 + s]]
            return 0

        lax.fori_loop(0, NX, one, 0, unroll=4)
        start_plane(
            lambda t: ps[n].at[t],
            lambda: boxes_out.at[c, :, pl.ds(pl.multiple_of(half * HALF + p * SHARE, SHARE), SHARE), :],
            p_sem.at[n],
            send_sem.at[2 * CHUNKS + n],
        )

    to_z(0)
    bt[...] = jnp.zeros_like(bt)
    for c in range(3):
        for k in range(PATCH_Z):
            bt[pl.ds(c * PATCH_Z + k, 32, stride=16), :] = m[c, k + 1, 8:40, :]
    columns = bt[...]
    new_row = new_ref[...]
    local_x = ax_ref[...] - p * 32
    local_y = ay_ref[...] - z * 128
    boxes = new_row.shape[1]
    depth = iota((128, boxes), 0)
    corners = [None] * 4
    for f in range(2):
        hot = jnp.where(depth == local_y + f, 1.0, 0.0)
        picked = jnp.dot(columns, hot, precision=PRECISE, preferred_element_type=F32)
        for e in range(2):
            total = jnp.zeros((16, boxes), F32)
            for x in range(32):
                here = jnp.where(local_x + e == x, 1.0, 0.0)
                total = total + picked[x * 16 : (x + 1) * 16] * here
            corners[e * 2 + f] = total
    terms = jnp.concatenate(corners, axis=0)
    odd = (new_row & 1).astype(F32)
    terms = jnp.concatenate([terms * (1.0 - odd), terms * odd], axis=0)
    owner = jnp.where((new_row >> 1) == iota((boxes, boxes), 0), 1.0, 0.0)
    ts[...] = dot_nt(owner, terms).reshape(NX, NZ, 128)
    start_plane(lambda t: ts.at[t], lambda: tr.at[p], t_sem, send_sem.at[3 * CHUNKS + 4])

    to_z(1)
    for at, (_, dst, _) in enumerate(halos):
        wait_all(dst, h_sem.at[at])
    for c in range(3):
        block = slice(c * 64, (c + 1) * 64)
        m[c, 1:65, 7, :] = jnp.where(p > 0, hxr[0, block, :], 0.0)
        m[c, 1:65, 40, :] = jnp.where(p < NX - 1, hxr[1, block, :], 0.0)
    stores = []
    for part in range(4):
        first, last = part * 16, part * 16 + 16
        meso_levels(m, hyr, mout, p, z, first, last)
        span = pl.ds(first, last - first)
        stores.append(pltpu.make_async_copy(mout.at[:, span], meso_out.at[:, span], local_sem.at[part]))
        stores[-1].start()
        to_z(part + 2)

    wait_all(tr, t_sem)
    summed = jnp.sum(tr[...], axis=0)
    for t in range(NZ):
        tz[t] = summed[t : t + 1]
    start_z(lambda t: tz.at[t], lambda: tzr.at[z], tz_sem, send_sem.at[3 * CHUNKS + 5])

    mine = (p * NZ + z) * 2
    hot = jnp.where(new_row == mine + iota((8, boxes), 0), 1.0, 0.0)
    px, py = pxy_ref[:, 0, :], pxy_ref[:, 1, :]
    pz, pc = pz_ref[...], pc_ref[...]
    points_out[...] = dot_nt(hot, jnp.concatenate([px, px, py, py, pz, pz, pc, pc], axis=0))
    fields = jnp.concatenate(
        [
            offset_ref[...].astype(F32),
            shift_ref[...].astype(F32),
            jnp.ones((1, boxes), F32),
            jnp.zeros((123, boxes), F32),
        ],
        axis=0,
    )
    ints_out[...] = jnp.round(dot_nt(hot, fields)).astype(I32)

    for n in range(CHUNKS):
        to_owner(n)
    wait_all(tzr, tz_sem)
    patch_out[...] = jnp.sum(tzr[...], axis=0)

    for store in stores:
        store.wait()
    for n in range(CHUNKS):
        wait_all(boxes_out.at[n // 2, :, pl.ds(n % 2 * HALF, HALF), :], p_sem.at[n])

    def sent(ref, sem):
        pltpu.make_async_remote_copy(
            ref, ref, sem, h_sem.at[0], device_id=device(p, z), device_id_type=MESH
        ).wait_send()

    for n in range(CHUNKS):
        sent(r[n].at[pl.ds(0, (NX - 1) * 16), :], send_sem.at[n])
        sent(zs[n].at[pl.ds(0, (NZ - 1) * places)], send_sem.at[CHUNKS + n])
        sent(ps[n].at[pl.ds(0, NX - 1)], send_sem.at[2 * CHUNKS + n])
    for at in range(4):
        sent(halos[at][0], send_sem.at[3 * CHUNKS + at])
    sent(ts.at[pl.ds(0, NX - 1)], send_sem.at[3 * CHUNKS + 4])
    sent(tz.at[pl.ds(0, NZ - 1)], send_sem.at[3 * CHUNKS + 5])


def split_pair(a):
    high = a.astype(jnp.bfloat16)
    return high, (a - high.astype(F32)).astype(jnp.bfloat16)


def gauss_line(distance):
    return jnp.exp(-((distance / KERNEL_WIDTH) ** 2)) / (math.sqrt(math.pi) * KERNEL_WIDTH)


def box_kernel(boxes, meso, patch, points, ints, out, meso_out, held, merged, load_sem, meso_sem):
    through = pltpu.make_async_copy(meso, meso_out, meso_sem)
    through.start()
    loads = []
    for s in range(2):
        for c in range(3):
            loads.append(
                pltpu.make_async_copy(
                    boxes.at[c, s], held.at[s, c, pl.ds(MARGIN, ROWS), :], load_sem.at[s * 3 + c]
                )
            )
            loads[-1].start()
    lane, h = iota((32, 128), 1), iota((32, 128), 0)
    i, j = 2 * h + (lane >> 6), lane & 63
    tall, wide = iota((128, 128), 0), iota((128, 128), 1)
    table = level_table()
    for s in range(2):
        ox, oy, sx, sy, occupied = [ints[s, at] for at in range(5)]
        flat = sx * 64 + sy
        rows, turn = flat >> 7, flat & 127
        valid = (i + sx >= 0) & (i + sx < 64) & (j + sy >= 0) & (j + sy < 64)
        right_x = ((ox + i).astype(F32) + 0.5) / RATIO
        right_y = ((oy + j).astype(F32) + 0.5) / RATIO
        left_x, left_y = 1.0 - right_x, 1.0 - right_y
        weights = [left_x * left_y, left_x * right_y, right_x * left_y, right_x * right_y]
        x_row = points[s : s + 1, 0:128]
        y_row = points[s : s + 1, 128:256]
        z_row = points[s : s + 1, 256:384]
        coef = points[s : s + 1, 384:512]
        kx = gauss_line((2 * iota((32, 128), 0) + (lane >> 6)).astype(F32) + 0.5 - x_row)
        kz = gauss_line(iota((BOX_Z, 128), 0).astype(F32) + 0.5 - z_row)
        ky = gauss_line((tall & 63).astype(F32) + 0.5 - y_row)
        ky = jnp.where((tall >> 6) == (wide >> 6), ky, 0.0)
        ky_high, ky_low = split_pair(ky)
        twice = jnp.concatenate([ky_high, ky_low], axis=1)
        sample_w = jnp.concatenate([twice, twice], axis=0)
        spread_w = jnp.concatenate(
            [jnp.concatenate([ky_high, ky_high], axis=1), jnp.concatenate([ky_low, ky_low], axis=1)], axis=0
        )
        samples = []
        for c in range(3):
            loads[s * 3 + c].wait()
            planes = []
            for k in range(PATCH_Z):
                plane = weights[0] * patch[0, s * 64 + c * PATCH_Z + k]
                for at in range(1, 4):
                    plane = plane + weights[at] * patch[0, s * 64 + at * 16 + c * PATCH_Z + k]
                planes.append(plane)
            for level in range(BOX_Z):
                below, part = table[level]
                fill = planes[below]
                if part:
                    fill = (1.0 - part) * fill + part * planes[below + 1]
                start = MARGIN + level * 32 + rows
                first = held[s, c, pl.ds(start, 32), :]
                second = held[s, c, pl.ds(start + 1, 32), :]
                moved = pltpu.roll(jnp.where(lane >= turn, first, second), 128 - turn, 1)
                merged[s, c, level * 32 : (level + 1) * 32, :] = jnp.where(valid, moved, fill)
            block = merged[s, c]
            high, low = split_pair(block)
            both = jnp.dot(
                jnp.concatenate([high, low], axis=1), sample_w, preferred_element_type=F32
            )
            sums = (both[:, :128] + both[:, 128:]).reshape(BOX_Z, 32, 128) * kx[None]
            per_level = jnp.sum(sums, axis=1) * kz
            half = jnp.sum(per_level, axis=0, keepdims=True)
            samples.append(half + pltpu.roll(half, 64, 1))
        magnitude = jnp.sqrt(1.0 + (samples[0] ** 2 + samples[1] ** 2 + samples[2] ** 2))
        shape = (kz[:, None, :] * kx[None]).reshape(ROWS, 128)
        for c in range(3):
            force = FORCE_GAIN * (-0.5 * coef * magnitude * samples[c])
            high, low = split_pair(shape * force)
            both = lax.dot_general(
                jnp.concatenate([high, low], axis=1),
                spread_w,
                (((1,), (1,)), ((), ())),
                preferred_element_type=F32,
            )
            finished = merged[s, c] + (both[:, :128] + both[:, 128:])
            out[c, pl.ds(s, ROWS, stride=2), :] = jnp.where(occupied > 0, finished, 0.0)
    through.wait()


def vmem():
    return pl.BlockSpec(memory_space=pltpu.VMEM)


def smem():
    return pl.BlockSpec(memory_space=pltpu.SMEM)


def anywhere():
    return pl.BlockSpec(memory_space=pl.ANY)


def exchange(places, collective_id, operands):
    shape = jax.ShapeDtypeStruct
    dma = pltpu.SemaphoreType.DMA
    return pl.pallas_call(
        functools.partial(exchange_kernel, places),
        out_shape=(
            shape((3, 2, ROWS, 128), F32),
            shape((3, 64, 32, 128), F32),
            shape((1, 128), F32),
            shape((8, 512), F32),
            shape((8, 128), I32),
        ),
        in_specs=[anywhere(), anywhere(), smem(), smem()] + [vmem()] * 8,
        out_specs=(anywhere(), anywhere(), vmem(), vmem(), vmem()),
        scratch_shapes=[
            (pltpu.VMEM((ROWS, 128), F32),) * CHUNKS,
            (pltpu.VMEM((2 * NX, SHARE, 128), F32),) * CHUNKS,
            (pltpu.VMEM((NZ * places, SHARE, 128), F32),) * CHUNKS,
            (pltpu.VMEM((NZ * places, SHARE, 128), F32),) * CHUNKS,
            (pltpu.VMEM((NX, 2, SHARE, 128), F32),) * CHUNKS,
            pltpu.VMEM((3, 66, 48, 128), F32),
            pltpu.VMEM((3, 64, 32, 128), F32),
            pltpu.VMEM((2, 192, 128), F32),
            pltpu.VMEM((2, 192, 128), F32),
            pltpu.VMEM((2, 32, 256), F32),
            pltpu.VMEM((2, 32, 256), F32),
            pltpu.VMEM((512, 128), F32),
            pltpu.VMEM((NX, NZ, 128), F32),
            pltpu.VMEM((NX, NZ, 128), F32),
            pltpu.VMEM((NZ, 1, 128), F32),
            pltpu.VMEM((NZ, 1, 128), F32),
            dma((3 * CHUNKS + 6,)),
            dma((CHUNKS,)),
            dma((CHUNKS,)),
            dma((CHUNKS,)),
            dma,
            dma,
            dma((4,)),
            dma((5,)),
        ],
        compiler_params=pltpu.CompilerParams(
            collective_id=collective_id, has_side_effects=True, vmem_limit_bytes=56 << 20
        ),
        name="exchange",
    )(*operands)


def local(
    meso_wind,
    old_boxes,
    box_old_slot,
    box_new_slot,
    anchor_x,
    anchor_y,
    box_offset,
    wind_shift,
    point_xy,
    point_z,
    point_coef,
):
    shape = jax.ShapeDtypeStruct
    old_row, new_row = box_old_slot.reshape(1, -1), box_new_slot.reshape(1, -1)
    send_tab, take_tab, choice = pl.pallas_call(
        tables_kernel,
        out_shape=(shape((1, NZ * PLACES), I32),) + (shape((1, 128), I32),) * 2,
        in_specs=[vmem(), vmem()],
        out_specs=(vmem(),) * 3,
        name="tables",
    )(old_row, new_row)
    old = jnp.transpose(old_boxes.reshape(2, 3, ROWS, 128), (1, 2, 0, 3)).reshape(3, 2 * ROWS, 128)
    operands = (
        old,
        meso_wind,
        send_tab,
        take_tab,
        new_row,
        anchor_x.reshape(1, -1),
        anchor_y.reshape(1, -1),
        box_offset.T,
        wind_shift.T,
        jnp.transpose(point_xy, (1, 2, 0)),
        point_z.T,
        point_coef.T,
    )
    boxes, meso_next, patch, points, ints = lax.switch(
        choice[0, 0],
        [functools.partial(exchange, size, at + 1) for at, size in enumerate(SIZES)],
        operands,
    )
    new_boxes, meso_next = pl.pallas_call(
        box_kernel,
        out_shape=(shape((3, 2 * ROWS, 128), F32), shape((3, 64, 32, 128), F32)),
        in_specs=[anywhere(), anywhere(), smem(), vmem(), smem()],
        out_specs=(vmem(), anywhere()),
        scratch_shapes=[
            pltpu.VMEM((2, 3, ROWS + 2 * MARGIN, 128), F32),
            pltpu.VMEM((2, 3, ROWS, 128), F32),
            pltpu.SemaphoreType.DMA((6,)),
            pltpu.SemaphoreType.DMA,
        ],
        compiler_params=pltpu.CompilerParams(vmem_limit_bytes=40 << 20),
        name="boxes",
    )(boxes, meso_next, patch, points, ints)
    new_boxes = jnp.transpose(new_boxes.reshape(3, ROWS, 2, 128), (2, 0, 1, 3)).reshape(2, 3, ROWS * 128)
    return (meso_next, new_boxes)


def solution(mesh):
    whole = P(("grp", "gx", "gy"), None, None)
    grid = P(None, None, ("grp", "gx"), "gy")
    return jax.shard_map(
        local,
        mesh=mesh,
        in_specs=(grid, whole) + (P(),) * 9,
        out_specs=(grid, whole),
        check_vma=False,
    )
```

```python
import functools
import math

import jax
import jax.numpy as jnp
import numpy as np
from jax import lax
from jax.experimental import pallas as pl
from jax.experimental.pallas import tpu as pltpu
from jax.sharding import PartitionSpec as P

MESH = pl.DeviceIdType.MESH
F32 = jnp.float32
I32 = jnp.int32
PRECISE = lax.Precision.HIGHEST
BOX_Z = 16
PATCH_Z = 5
RATIO = 100
TIME_STEP = 0.2
VISCOSITY = 0.1
KERNEL_WIDTH = 2.0
FORCE_GAIN = 20.0
NX, NZ = 32, 8
PLACES = 64
SIZES = (8, 9, 10, 12, PLACES)
ROWS = 512
CHUNKS = 6
HALF = ROWS // 2
SHARE = HALF // NX
MARGIN = 16


def level_table():
    table = []
    for level in range(BOX_Z):
        height = max((level - 1.5) / 4.0, 0.0)
        below = int(math.floor(height))
        table.append((below, height - below))
    return table


def position():
    grp, gx, z = lax.axis_index("grp"), lax.axis_index("gx"), lax.axis_index("gy")
    return grp * 16 + gx, z


def device(p, z):
    return (p // 16, lax.rem(p, 16), z)


def iota(shape, dim):
    return lax.broadcasted_iota(I32, shape, dim)


def dot_nt(a, b):
    return lax.dot_general(a, b, (((1,), (1,)), ((), ())), precision=PRECISE, preferred_element_type=F32)


def tables_kernel(old_ref, new_ref, send_ref, take_ref, choice_ref):
    z = lax.axis_index("gy")
    boxes = old_ref.shape[1]
    old_row, new_row = old_ref[...], new_ref[...]
    across, down = iota((boxes, boxes), 1), iota((boxes, boxes), 0)
    same = across == down

    def column(row):
        return jnp.sum(jnp.where(same, row.astype(F32), 0.0), axis=1, keepdims=True).astype(I32)

    old_col, new_col = column(old_row), column(new_row)
    z_old, z_new = (old_col >> 1) & 7, (new_col >> 1) & 7
    pair_col = z_old * NZ + z_new
    pair_row = ((old_row >> 1) & 7) * NZ + ((new_row >> 1) & 7)
    before = (pair_row == pair_col) & (across < down)
    rank_f = jnp.sum(jnp.where(before, 1.0, 0.0), axis=1, keepdims=True)
    rank = rank_f.astype(I32)
    old_local = (old_col >> 4) * 2 + (old_col & 1)
    new_local = (new_col >> 4) * 2 + (new_col & 1)
    sends = jnp.where(z_old == z, z_new * PLACES + rank, -1)
    takes = jnp.where(z_new == z, new_local, -1)
    send_hot = iota((boxes, NZ * PLACES), 1) == sends
    take_hot = iota((boxes, 128), 1) == takes
    send_ref[...] = jnp.sum(
        jnp.where(send_hot, old_local.astype(F32), 0.0), axis=0, keepdims=True
    ).astype(I32)
    most = jnp.max(rank_f, axis=0, keepdims=True)
    limit = jnp.full((1, 1), SIZES[0], F32)
    choice = jnp.zeros((1, 1), F32)
    for at, size in enumerate(SIZES[1:]):
        full = most >= SIZES[at]
        limit, choice = jnp.where(full, float(size), limit), jnp.where(full, at + 1.0, choice)
    place = z_old.astype(F32) * limit + rank_f
    take_ref[...] = jnp.sum(jnp.where(take_hot, place, 0.0), axis=0, keepdims=True).astype(I32)
    choice_ref[...] = jnp.broadcast_to(choice, (1, 128)).astype(I32)


def meso_levels(m, halo_y, mout, p, z, first, last):
    lane = iota((32, 128), 1)
    has_south, has_north = z > 0, z < NZ - 1

    def level(k, _):
        winds = [m[c, k + 1, 8:40, :] for c in range(3)]
        u, v, w = winds
        for c in range(3):
            q = winds[c]
            west, east = m[c, k + 1, 7:39, :], m[c, k + 1, 9:41, :]
            below, above = m[c, k, 8:40, :], m[c, k + 2, 8:40, :]
            tile = 128 if c == 2 else 0
            at = k + (64 if c == 1 else 0)
            south_edge = pltpu.roll(halo_y[0, :, tile : tile + 128], 128 - at, 1)
            north_edge = pltpu.roll(halo_y[1, :, tile : tile + 128], 127 - at, 1)
            south_edge = jnp.where(has_south, south_edge, 0.0)
            north_edge = jnp.where(has_north, north_edge, 0.0)
            south = jnp.where(lane == 0, south_edge, pltpu.roll(q, 1, 1))
            north = jnp.where(lane == 127, north_edge, pltpu.roll(q, 127, 1))
            advect = u * jnp.where(u > 0, q - west, east - q)
            advect = advect + v * jnp.where(v > 0, q - south, north - q)
            advect = advect + w * jnp.where(w > 0, q - below, above - q)
            laplace = west + east + south + north + below + above - 6.0 * q
            mout[c, k] = q - TIME_STEP * advect + TIME_STEP * VISCOSITY * laplace
        return 0

    lax.fori_loop(first, last, level, 0)


def exchange_kernel(
    places,
    old,
    meso,
    send_tab,
    take_tab,
    new_ref,
    ax_ref,
    ay_ref,
    offset_ref,
    shift_ref,
    pxy_ref,
    pz_ref,
    pc_ref,
    boxes_out,
    meso_out,
    patch_out,
    points_out,
    ints_out,
    r,
    rd,
    zs,
    zr,
    ps,
    m,
    mout,
    hxs,
    hxr,
    hys,
    hyr,
    bt,
    ts,
    tr,
    tz,
    tzr,
    send_sem,
    a_sem,
    z_sem,
    p_sem,
    t_sem,
    tz_sem,
    h_sem,
    local_sem,
):
    p, z = position()
    barrier = pltpu.get_barrier_semaphore()

    def greet_z(d, _):
        pl.semaphore_signal(
            barrier, inc=1, device_id=device(p, lax.rem(z + d, NZ)), device_id_type=MESH
        )
        return 0

    def greet_plane(d, _):
        pl.semaphore_signal(
            barrier, inc=1, device_id=device(lax.rem(p + d, NX), z), device_id_type=MESH
        )
        return 0

    lax.fori_loop(1, NZ, greet_z, 0)
    lax.fori_loop(1, NX, greet_plane, 0)

    load = pltpu.make_async_copy(meso, m.at[:, pl.ds(1, 64), pl.ds(8, 32), :], local_sem.at[4])
    load.start()
    pl.semaphore_wait(barrier, NX + NZ - 2)

    def start_plane(src_of, dst_of, recv, sent):
        def one(d, _):
            t = lax.rem(p + d, NX)
            pltpu.make_async_remote_copy(
                src_of(t), dst_of(), sent, recv, device_id=device(t, z), device_id_type=MESH
            ).start()
            return 0

        lax.fori_loop(1, NX, one, 0)
        pltpu.make_async_copy(src_of(p), dst_of(), recv).start()

    def start_z(src_of, dst_of, recv, sent):
        def one(d, _):
            t = lax.rem(z + d, NZ)
            pltpu.make_async_remote_copy(
                src_of(t), dst_of(), sent, recv, device_id=device(p, t), device_id_type=MESH
            ).start()
            return 0

        lax.fori_loop(1, NZ, one, 0)
        pltpu.make_async_copy(src_of(z), dst_of(), recv).start()

    def wait_all(ref, sem):
        pltpu.make_async_copy(ref, ref, sem).wait()

    def spread(n):
        c, half = n // 2, n % 2
        start_plane(
            lambda t: old.at[c, pl.ds(pl.multiple_of(half * 2 * HALF + t * 16, 16), 16), :],
            lambda: r[n].at[pl.ds(pl.multiple_of(p * 16, 16), 16), :],
            a_sem.at[n],
            send_sem.at[n],
        )

    spread(0)
    for n in range(1, CHUNKS):
        spread(n)

    zero_level = jnp.zeros((48, 128), F32)
    for c in range(3):
        m[c, 0] = zero_level
        m[c, 65] = zero_level
    load.wait()

    for c in range(3):
        hxs[0, c * 64 : (c + 1) * 64, :] = m[c, 1:65, 39, :]
        hxs[1, c * 64 : (c + 1) * 64, :] = m[c, 1:65, 8, :]
    lane = iota((32, 128), 1)

    def pack(k, held):
        top0, top1, low0, low1 = held
        for c in range(3):
            q = m[c, k + 1, 8:40, :]
            at = k + (64 if c == 1 else 0)
            here = lane == at
            top = pltpu.roll(q, at + 1, 1)
            low = pltpu.roll(q, at, 1)
            if c < 2:
                top0, low0 = jnp.where(here, top, top0), jnp.where(here, low, low0)
            else:
                top1, low1 = jnp.where(here, top, top1), jnp.where(here, low, low1)
        return top0, top1, low0, low1

    blank = jnp.zeros((32, 128), F32)
    top0, top1, low0, low1 = lax.fori_loop(0, 64, pack, (blank, blank, blank, blank))
    hys[0, :, 0:128] = top0
    hys[0, :, 128:256] = top1
    hys[1, :, 0:128] = low0
    hys[1, :, 128:256] = low1
    halos = [
        (hxs.at[0], hxr.at[0], device(lax.rem(p + 1, NX), z)),
        (hxs.at[1], hxr.at[1], device(lax.rem(p + NX - 1, NX), z)),
        (hys.at[0], hyr.at[0], device(p, lax.rem(z + 1, NZ))),
        (hys.at[1], hyr.at[1], device(p, lax.rem(z + NZ - 1, NZ))),
    ]
    for at, (src, dst, target) in enumerate(halos):
        pltpu.make_async_remote_copy(
            src, dst, send_sem.at[3 * CHUNKS + at], h_sem.at[at], device_id=target, device_id_type=MESH
        ).start()

    def to_z(n):
        wait_all(r[n], a_sem.at[n])

        def part_slots(t, _):
            for s in range(2):
                rd[n][t * 2 + s] = r[n][pl.ds(pl.multiple_of(t * 16, 16) + s, 8, stride=2), :]
            return 0

        lax.fori_loop(0, NX, part_slots, 0, unroll=4)

        def one(e, _):
            zt, q = e // places, lax.rem(e, places)
            zs[n][e] = rd[n][send_tab[0, zt * PLACES + q]]
            return 0

        lax.fori_loop(0, NZ * places, one, 0, unroll=4)
        start_z(
            lambda t: zs[n].at[pl.ds(t * places, places)],
            lambda: zr[n].at[pl.ds(z * places, places)],
            z_sem.at[n],
            send_sem.at[CHUNKS + n],
        )

    def to_owner(n):
        c, half = n // 2, n % 2
        wait_all(zr[n], z_sem.at[n])

        def one(t, _):
            for s in range(2):
                ps[n][t, s] = zr[n][take_tab[0, t * 2 + s]]
            return 0

        lax.fori_loop(0, NX, one, 0, unroll=4)
        start_plane(
            lambda t: ps[n].at[t],
            lambda: boxes_out.at[c, :, pl.ds(pl.multiple_of(half * HALF + p * SHARE, SHARE), SHARE), :],
            p_sem.at[n],
            send_sem.at[2 * CHUNKS + n],
        )

    to_z(0)
    bt[...] = jnp.zeros_like(bt)
    for c in range(3):
        for k in range(PATCH_Z):
            bt[pl.ds(c * PATCH_Z + k, 32, stride=16), :] = m[c, k + 1, 8:40, :]
    columns = bt[...]
    new_row = new_ref[...]
    local_x = ax_ref[...] - p * 32
    local_y = ay_ref[...] - z * 128
    boxes = new_row.shape[1]
    depth = iota((128, boxes), 0)
    corners = [None] * 4
    for f in range(2):
        hot = jnp.where(depth == local_y + f, 1.0, 0.0)
        picked = jnp.dot(columns, hot, precision=PRECISE, preferred_element_type=F32)
        for e in range(2):
            total = jnp.zeros((16, boxes), F32)
            for x in range(32):
                here = jnp.where(local_x + e == x, 1.0, 0.0)
                total = total + picked[x * 16 : (x + 1) * 16] * here
            corners[e * 2 + f] = total
    terms = jnp.concatenate(corners, axis=0)
    odd = (new_row & 1).astype(F32)
    terms = jnp.concatenate([terms * (1.0 - odd), terms * odd], axis=0)
    owner = jnp.where((new_row >> 1) == iota((boxes, boxes), 0), 1.0, 0.0)
    ts[...] = dot_nt(owner, terms).reshape(NX, NZ, 128)
    start_plane(lambda t: ts.at[t], lambda: tr.at[p], t_sem, send_sem.at[3 * CHUNKS + 4])

    to_z(1)
    for at, (_, dst, _) in enumerate(halos):
        wait_all(dst, h_sem.at[at])
    for c in range(3):
        block = slice(c * 64, (c + 1) * 64)
        m[c, 1:65, 7, :] = jnp.where(p > 0, hxr[0, block, :], 0.0)
        m[c, 1:65, 40, :] = jnp.where(p < NX - 1, hxr[1, block, :], 0.0)
    stores = []
    for part in range(4):
        first, last = part * 16, part * 16 + 16
        meso_levels(m, hyr, mout, p, z, first, last)
        span = pl.ds(first, last - first)
        stores.append(pltpu.make_async_copy(mout.at[:, span], meso_out.at[:, span], local_sem.at[part]))
        stores[-1].start()
        to_z(part + 2)

    wait_all(tr, t_sem)
    summed = jnp.sum(tr[...], axis=0)
    for t in range(NZ):
        tz[t] = summed[t : t + 1]
    start_z(lambda t: tz.at[t], lambda: tzr.at[z], tz_sem, send_sem.at[3 * CHUNKS + 5])

    mine = (p * NZ + z) * 2
    hot = jnp.where(new_row == mine + iota((8, boxes), 0), 1.0, 0.0)
    px, py = pxy_ref[:, 0, :], pxy_ref[:, 1, :]
    pz, pc = pz_ref[...], pc_ref[...]
    points_out[...] = dot_nt(hot, jnp.concatenate([px, px, py, py, pz, pz, pc, pc], axis=0))
    fields = jnp.concatenate(
        [
            offset_ref[...].astype(F32),
            shift_ref[...].astype(F32),
            jnp.ones((1, boxes), F32),
            jnp.zeros((123, boxes), F32),
        ],
        axis=0,
    )
    ints_out[...] = jnp.round(dot_nt(hot, fields)).astype(I32)

    for n in range(CHUNKS):
        to_owner(n)
    wait_all(tzr, tz_sem)
    patch_out[...] = jnp.sum(tzr[...], axis=0)

    for store in stores:
        store.wait()
    for n in range(CHUNKS):
        wait_all(boxes_out.at[n // 2, :, pl.ds(n % 2 * HALF, HALF), :], p_sem.at[n])

    def sent(ref, sem):
        pltpu.make_async_remote_copy(
            ref, ref, sem, h_sem.at[0], device_id=device(p, z), device_id_type=MESH
        ).wait_send()

    for n in range(CHUNKS):
        sent(r[n].at[pl.ds(0, (NX - 1) * 16), :], send_sem.at[n])
        sent(zs[n].at[pl.ds(0, (NZ - 1) * places)], send_sem.at[CHUNKS + n])
        sent(ps[n].at[pl.ds(0, NX - 1)], send_sem.at[2 * CHUNKS + n])
    for at in range(4):
        sent(halos[at][0], send_sem.at[3 * CHUNKS + at])
    sent(ts.at[pl.ds(0, NX - 1)], send_sem.at[3 * CHUNKS + 4])
    sent(tz.at[pl.ds(0, NZ - 1)], send_sem.at[3 * CHUNKS + 5])


def split_pair(a):
    high = a.astype(jnp.bfloat16)
    return high, (a - high.astype(F32)).astype(jnp.bfloat16)


def gauss_line(distance):
    return jnp.exp(-((distance / KERNEL_WIDTH) ** 2)) / (math.sqrt(math.pi) * KERNEL_WIDTH)


def box_kernel(boxes, meso, patch, points, ints, out, meso_out, held, merged, load_sem, meso_sem):
    through = pltpu.make_async_copy(meso, meso_out, meso_sem)
    through.start()
    loads = []
    for s in range(2):
        for c in range(3):
            loads.append(
                pltpu.make_async_copy(
                    boxes.at[c, s], held.at[s, c, pl.ds(MARGIN, ROWS), :], load_sem.at[s * 3 + c]
                )
            )
            loads[-1].start()
    lane, h = iota((32, 128), 1), iota((32, 128), 0)
    i, j = 2 * h + (lane >> 6), lane & 63
    tall, wide = iota((128, 128), 0), iota((128, 128), 1)
    table = level_table()
    for s in range(2):
        ox, oy, sx, sy, occupied = [ints[s, at] for at in range(5)]
        flat = sx * 64 + sy
        rows, turn = flat >> 7, flat & 127
        valid = (i + sx >= 0) & (i + sx < 64) & (j + sy >= 0) & (j + sy < 64)
        right_x = ((ox + i).astype(F32) + 0.5) / RATIO
        right_y = ((oy + j).astype(F32) + 0.5) / RATIO
        left_x, left_y = 1.0 - right_x, 1.0 - right_y
        weights = [left_x * left_y, left_x * right_y, right_x * left_y, right_x * right_y]
        x_row = points[s : s + 1, 0:128]
        y_row = points[s : s + 1, 128:256]
        z_row = points[s : s + 1, 256:384]
        coef = points[s : s + 1, 384:512]
        kx = gauss_line((2 * iota((32, 128), 0) + (lane >> 6)).astype(F32) + 0.5 - x_row)
        kz = gauss_line(iota((BOX_Z, 128), 0).astype(F32) + 0.5 - z_row)
        ky = gauss_line((tall & 63).astype(F32) + 0.5 - y_row)
        ky = jnp.where((tall >> 6) == (wide >> 6), ky, 0.0)
        ky_high, ky_low = split_pair(ky)
        twice = jnp.concatenate([ky_high, ky_low], axis=1)
        sample_w = jnp.concatenate([twice, twice], axis=0)
        spread_w = jnp.concatenate(
            [jnp.concatenate([ky_high, ky_high], axis=1), jnp.concatenate([ky_low, ky_low], axis=1)], axis=0
        )
        samples = []
        for c in range(3):
            loads[s * 3 + c].wait()
            planes = []
            for k in range(PATCH_Z):
                plane = weights[0] * patch[0, s * 64 + c * PATCH_Z + k]
                for at in range(1, 4):
                    plane = plane + weights[at] * patch[0, s * 64 + at * 16 + c * PATCH_Z + k]
                planes.append(plane)
            for level in range(BOX_Z):
                below, part = table[level]
                fill = planes[below]
                if part:
                    fill = (1.0 - part) * fill + part * planes[below + 1]
                start = MARGIN + level * 32 + rows
                first = held[s, c, pl.ds(start, 32), :]
                second = held[s, c, pl.ds(start + 1, 32), :]
                moved = pltpu.roll(jnp.where(lane >= turn, first, second), 128 - turn, 1)
                merged[s, c, level * 32 : (level + 1) * 32, :] = jnp.where(valid, moved, fill)
            block = merged[s, c]
            high, low = split_pair(block)
            both = jnp.dot(
                jnp.concatenate([high, low], axis=1), sample_w, preferred_element_type=F32
            )
            sums = (both[:, :128] + both[:, 128:]).reshape(BOX_Z, 32, 128) * kx[None]
            per_level = jnp.sum(sums, axis=1) * kz
            half = jnp.sum(per_level, axis=0, keepdims=True)
            samples.append(half + pltpu.roll(half, 64, 1))
        magnitude = jnp.sqrt(1.0 + (samples[0] ** 2 + samples[1] ** 2 + samples[2] ** 2))
        shape = (kz[:, None, :] * kx[None]).reshape(ROWS, 128)
        for c in range(3):
            force = FORCE_GAIN * (-0.5 * coef * magnitude * samples[c])
            high, low = split_pair(shape * force)
            both = lax.dot_general(
                jnp.concatenate([high, low], axis=1),
                spread_w,
                (((1,), (1,)), ((), ())),
                preferred_element_type=F32,
            )
            finished = merged[s, c] + (both[:, :128] + both[:, 128:])
            out[c, pl.ds(s, ROWS, stride=2), :] = jnp.where(occupied > 0, finished, 0.0)
    through.wait()


def vmem():
    return pl.BlockSpec(memory_space=pltpu.VMEM)


def smem():
    return pl.BlockSpec(memory_space=pltpu.SMEM)


def anywhere():
    return pl.BlockSpec(memory_space=pl.ANY)


def exchange(places, collective_id, operands):
    shape = jax.ShapeDtypeStruct
    dma = pltpu.SemaphoreType.DMA
    return pl.pallas_call(
        functools.partial(exchange_kernel, places),
        out_shape=(
            shape((3, 2, ROWS, 128), F32),
            shape((3, 64, 32, 128), F32),
            shape((1, 128), F32),
            shape((8, 512), F32),
            shape((8, 128), I32),
        ),
        in_specs=[anywhere(), anywhere(), smem(), smem()] + [vmem()] * 8,
        out_specs=(anywhere(), anywhere(), vmem(), vmem(), vmem()),
        scratch_shapes=[
            (pltpu.VMEM((ROWS, 128), F32),) * CHUNKS,
            (pltpu.VMEM((2 * NX, SHARE, 128), F32),) * CHUNKS,
            (pltpu.VMEM((NZ * places, SHARE, 128), F32),) * CHUNKS,
            (pltpu.VMEM((NZ * places, SHARE, 128), F32),) * CHUNKS,
            (pltpu.VMEM((NX, 2, SHARE, 128), F32),) * CHUNKS,
            pltpu.VMEM((3, 66, 48, 128), F32),
            pltpu.VMEM((3, 64, 32, 128), F32),
            pltpu.VMEM((2, 192, 128), F32),
            pltpu.VMEM((2, 192, 128), F32),
            pltpu.VMEM((2, 32, 256), F32),
            pltpu.VMEM((2, 32, 256), F32),
            pltpu.VMEM((512, 128), F32),
            pltpu.VMEM((NX, NZ, 128), F32),
            pltpu.VMEM((NX, NZ, 128), F32),
            pltpu.VMEM((NZ, 1, 128), F32),
            pltpu.VMEM((NZ, 1, 128), F32),
            dma((3 * CHUNKS + 6,)),
            dma((CHUNKS,)),
            dma((CHUNKS,)),
            dma((CHUNKS,)),
            dma,
            dma,
            dma((4,)),
            dma((5,)),
        ],
        compiler_params=pltpu.CompilerParams(
            collective_id=collective_id, has_side_effects=True, vmem_limit_bytes=56 << 20
        ),
        name="exchange",
    )(*operands)


def local(
    meso_wind,
    old_boxes,
    box_old_slot,
    box_new_slot,
    anchor_x,
    anchor_y,
    box_offset,
    wind_shift,
    point_xy,
    point_z,
    point_coef,
):
    shape = jax.ShapeDtypeStruct
    old_row, new_row = box_old_slot.reshape(1, -1), box_new_slot.reshape(1, -1)
    send_tab, take_tab, choice = pl.pallas_call(
        tables_kernel,
        out_shape=(shape((1, NZ * PLACES), I32),) + (shape((1, 128), I32),) * 2,
        in_specs=[vmem(), vmem()],
        out_specs=(vmem(),) * 3,
        name="tables",
    )(old_row, new_row)
    old = jnp.transpose(old_boxes.reshape(2, 3, ROWS, 128), (1, 2, 0, 3)).reshape(3, 2 * ROWS, 128)
    operands = (
        old,
        meso_wind,
        send_tab,
        take_tab,
        new_row,
        anchor_x.reshape(1, -1),
        anchor_y.reshape(1, -1),
        box_offset.T,
        wind_shift.T,
        jnp.transpose(point_xy, (1, 2, 0)),
        point_z.T,
        point_coef.T,
    )
    boxes, meso_next, patch, points, ints = lax.switch(
        choice[0, 0],
        [functools.partial(exchange, size, at + 1) for at, size in enumerate(SIZES)],
        operands,
    )
    new_boxes, meso_next = pl.pallas_call(
        box_kernel,
        out_shape=(shape((3, 2 * ROWS, 128), F32), shape((3, 64, 32, 128), F32)),
        in_specs=[anywhere(), anywhere(), smem(), vmem(), smem()],
        out_specs=(vmem(), anywhere()),
        scratch_shapes=[
            pltpu.VMEM((2, 3, ROWS + 2 * MARGIN, 128), F32),
            pltpu.VMEM((2, 3, ROWS, 128), F32),
            pltpu.SemaphoreType.DMA((6,)),
            pltpu.SemaphoreType.DMA,
        ],
        compiler_params=pltpu.CompilerParams(vmem_limit_bytes=40 << 20),
        name="boxes",
    )(boxes, meso_next, patch, points, ints)
    new_boxes = jnp.transpose(new_boxes.reshape(3, ROWS, 2, 128), (2, 0, 1, 3)).reshape(2, 3, ROWS * 128)
    return (meso_next, new_boxes)


def solution(mesh):
    whole = P(("grp", "gx", "gy"), None, None)
    grid = P(None, None, ("grp", "gx"), "gy")
    return jax.shard_map(
        local,
        mesh=mesh,
        in_specs=(grid, whole) + (P(),) * 9,
        out_specs=(grid, whole),
        check_vma=False,
    )
```

```python
import functools
import math

import jax
import jax.numpy as jnp
import numpy as np
from jax import lax
from jax.experimental import pallas as pl
from jax.experimental.pallas import tpu as pltpu
from jax.sharding import PartitionSpec as P

MESH = pl.DeviceIdType.MESH
F32 = jnp.float32
I32 = jnp.int32
PRECISE = lax.Precision.HIGHEST
BOX_Z = 16
PATCH_Z = 5
RATIO = 100
TIME_STEP = 0.2
VISCOSITY = 0.1
KERNEL_WIDTH = 2.0
FORCE_GAIN = 20.0
NX, NZ = 32, 8
PLACES = 64
SPILL = 16
PLANS = (((12, 6, 5, 5, 4), 8), ((16, 6, 6, 5, 4), 16), ((PLACES,) * 5, 0))
ROWS = 512
CHUNKS = 6
HALF = ROWS // 2
SHARE = HALF // NX
MARGIN = 16


def level_table():
    table = []
    for level in range(BOX_Z):
        height = max((level - 1.5) / 4.0, 0.0)
        below = int(math.floor(height))
        table.append((below, height - below))
    return table


def position():
    grp, gx, z = lax.axis_index("grp"), lax.axis_index("gx"), lax.axis_index("gy")
    return grp * 16 + gx, z


def device(p, z):
    return (p // 16, lax.rem(p, 16), z)


def iota(shape, dim):
    return lax.broadcasted_iota(I32, shape, dim)


def dot_nt(a, b):
    return lax.dot_general(a, b, (((1,), (1,)), ((), ())), precision=PRECISE, preferred_element_type=F32)


def places_of(caps):
    sizes = [caps[min(d, NZ - d)] for d in range(NZ)]
    starts = [sum(sizes[:d]) for d in range(NZ)]
    return sizes, starts, sum(sizes)


def by_value(index, values):
    found = jnp.zeros(index.shape, F32)
    for at, value in enumerate(values):
        found = jnp.where(index == at, float(value), found)
    return found


def tables_kernel(old_ref, new_ref, send_ref, spill_ref, relay_ref, take_ref, choice_ref):
    z = lax.axis_index("gy")
    boxes = old_ref.shape[1]
    old_row, new_row = old_ref[...], new_ref[...]
    across, down = iota((boxes, boxes), 1), iota((boxes, boxes), 0)
    same = across == down

    def column(row):
        return jnp.sum(jnp.where(same, row.astype(F32), 0.0), axis=1, keepdims=True).astype(I32)

    def count(mask, axis):
        return jnp.sum(jnp.where(mask, 1.0, 0.0), axis=axis, keepdims=True)

    old_col, new_col = column(old_row), column(new_row)
    from_col, to_col = (old_col >> 1) & 7, (new_col >> 1) & 7
    from_row, to_row = (old_row >> 1) & 7, (new_row >> 1) & 7
    same_from, same_to = from_row == from_col, to_row == to_col
    pair = same_from & same_to
    rank_col, rank_row = count(pair & (across < down), 1), count(pair & (down < across), 0)
    way_col, way_row = (to_col - from_col) & 7, (to_row - from_row) & 7
    choice = jnp.full((1, 1), len(PLANS) - 1, I32)
    sizes, starts, total = places_of(PLANS[-1][0])
    place = by_value(way_col, starts) + rank_col
    leaves = jnp.full((boxes, 1), -1.0, F32)
    enters = leaves
    relay = leaves
    for at in range(len(PLANS) - 2, -1, -1):
        caps, spill = PLANS[at]
        sizes, starts, total = places_of(caps)
        over_col, over_row = rank_col >= by_value(way_col, sizes), rank_row >= by_value(way_row, sizes)
        earlier = over_row & (across < down)
        out = jnp.where(over_col, count(earlier & same_from, 1), -1.0)
        into = jnp.where(over_col, count(earlier & same_to, 1), -1.0)
        fits = jnp.max(jnp.maximum(out, into), axis=0, keepdims=True) < spill
        direct = by_value(way_col, starts) + rank_col
        choice = jnp.where(fits, at, choice)
        place = jnp.where(fits, jnp.where(over_col, total + into, direct), place)
        leaves, enters = jnp.where(fits, out, leaves), jnp.where(fits, into, enters)
        relay = jnp.where(fits, from_col.astype(F32) * spill + out, relay)
    old_local = ((old_col >> 4) * 2 + (old_col & 1)).astype(F32)
    new_local = (new_col >> 4) * 2 + (new_col & 1)

    def table(size, key, value):
        hot = iota((boxes, size), 1) == key
        return jnp.sum(jnp.where(hot, value, 0.0), axis=0, keepdims=True).astype(I32)

    here = from_col == z
    send_ref[...] = table(NZ * PLACES, jnp.where(here, to_col * PLACES + rank_col.astype(I32), -1), old_local)
    spill_ref[...] = table(128, jnp.where(here, leaves.astype(I32), -1), old_local)
    relay_ref[...] = table(128, jnp.where(enters >= 0, to_col * SPILL + enters.astype(I32), -1), relay)
    take_ref[...] = table(128, jnp.where(to_col == z, new_local, -1), place)
    choice_ref[...] = jnp.broadcast_to(choice, (1, 128))


def meso_levels(m, halo_y, mout, p, z, first, last):
    lane = iota((32, 128), 1)
    has_south, has_north = z > 0, z < NZ - 1

    def level(k, _):
        winds = [m[c, k + 1, 8:40, :] for c in range(3)]
        u, v, w = winds
        for c in range(3):
            q = winds[c]
            west, east = m[c, k + 1, 7:39, :], m[c, k + 1, 9:41, :]
            below, above = m[c, k, 8:40, :], m[c, k + 2, 8:40, :]
            tile = 128 if c == 2 else 0
            at = k + (64 if c == 1 else 0)
            south_edge = pltpu.roll(halo_y[0, :, tile : tile + 128], 128 - at, 1)
            north_edge = pltpu.roll(halo_y[1, :, tile : tile + 128], 127 - at, 1)
            south_edge = jnp.where(has_south, south_edge, 0.0)
            north_edge = jnp.where(has_north, north_edge, 0.0)
            south = jnp.where(lane == 0, south_edge, pltpu.roll(q, 1, 1))
            north = jnp.where(lane == 127, north_edge, pltpu.roll(q, 127, 1))
            advect = u * jnp.where(u > 0, q - west, east - q)
            advect = advect + v * jnp.where(v > 0, q - south, north - q)
            advect = advect + w * jnp.where(w > 0, q - below, above - q)
            laplace = west + east + south + north + below + above - 6.0 * q
            mout[c, k] = q - TIME_STEP * advect + TIME_STEP * VISCOSITY * laplace
        return 0

    lax.fori_loop(first, last, level, 0)


def exchange_kernel(
    plan,
    old,
    meso,
    send_tab,
    spill_tab,
    relay_tab,
    take_tab,
    new_ref,
    ax_ref,
    ay_ref,
    offset_ref,
    shift_ref,
    pxy_ref,
    pz_ref,
    pc_ref,
    boxes_out,
    meso_out,
    patch_out,
    points_out,
    ints_out,
    r,
    rd,
    zs,
    zr,
    v1s,
    v1r,
    v2s,
    v2r,
    ps,
    m,
    mout,
    hxs,
    hxr,
    hys,
    hyr,
    bt,
    ts,
    tr,
    tz,
    tzr,
    send_sem,
    a_sem,
    z_sem,
    v1_sem,
    v2_sem,
    p_sem,
    t_sem,
    tz_sem,
    h_sem,
    local_sem,
):
    p, z = position()
    sizes, starts, total_places = places_of(plan[0])
    spill = plan[1]
    barrier = pltpu.get_barrier_semaphore()

    def greet_z(d, _):
        pl.semaphore_signal(
            barrier, inc=1, device_id=device(p, lax.rem(z + d, NZ)), device_id_type=MESH
        )
        return 0

    def greet_plane(d, _):
        pl.semaphore_signal(
            barrier, inc=1, device_id=device(lax.rem(p + d, NX), z), device_id_type=MESH
        )
        return 0

    lax.fori_loop(1, NZ, greet_z, 0)
    lax.fori_loop(1, NX, greet_plane, 0)

    load = pltpu.make_async_copy(meso, m.at[:, pl.ds(1, 64), pl.ds(8, 32), :], local_sem.at[4])
    load.start()
    zero_level = jnp.zeros((48, 128), F32)
    for c in range(3):
        m[c, 0] = zero_level
        m[c, 65] = zero_level
    load.wait()

    for c in range(3):
        hxs[0, c * 64 : (c + 1) * 64, :] = m[c, 1:65, 39, :]
        hxs[1, c * 64 : (c + 1) * 64, :] = m[c, 1:65, 8, :]
    lane = iota((32, 128), 1)

    def pack(k, held):
        top0, top1, low0, low1 = held
        for c in range(3):
            q = m[c, k + 1, 8:40, :]
            at = k + (64 if c == 1 else 0)
            here = lane == at
            top = pltpu.roll(q, at + 1, 1)
            low = pltpu.roll(q, at, 1)
            if c < 2:
                top0, low0 = jnp.where(here, top, top0), jnp.where(here, low, low0)
            else:
                top1, low1 = jnp.where(here, top, top1), jnp.where(here, low, low1)
        return top0, top1, low0, low1

    blank = jnp.zeros((32, 128), F32)
    top0, top1, low0, low1 = lax.fori_loop(0, 64, pack, (blank, blank, blank, blank))
    hys[0, :, 0:128] = top0
    hys[0, :, 128:256] = top1
    hys[1, :, 0:128] = low0
    hys[1, :, 128:256] = low1

    pl.semaphore_wait(barrier, NX + NZ - 2)

    def start_plane(src_of, dst_of, recv, sent):
        def one(d, _):
            t = lax.rem(p + d, NX)
            pltpu.make_async_remote_copy(
                src_of(t), dst_of(), sent, recv, device_id=device(t, z), device_id_type=MESH
            ).start()
            return 0

        lax.fori_loop(1, NX, one, 0)
        pltpu.make_async_copy(src_of(p), dst_of(), recv).start()

    def start_z(src_of, dst_of, recv, sent):
        def one(d, _):
            t = lax.rem(z + d, NZ)
            pltpu.make_async_remote_copy(
                src_of(t), dst_of(), sent, recv, device_id=device(p, t), device_id_type=MESH
            ).start()
            return 0

        lax.fori_loop(1, NZ, one, 0)
        pltpu.make_async_copy(src_of(z), dst_of(), recv).start()

    def wait_all(ref, sem):
        pltpu.make_async_copy(ref, ref, sem).wait()

    def spread(n):
        c, half = n // 2, n % 2
        start_plane(
            lambda t: old.at[c, pl.ds(pl.multiple_of(half * 2 * HALF + t * 16, 16), 16), :],
            lambda: r[n].at[pl.ds(pl.multiple_of(p * 16, 16), 16), :],
            a_sem.at[n],
            send_sem.at[n],
        )

    spread(0)
    halos = [
        (hxs.at[0], hxr.at[0], device(lax.rem(p + 1, NX), z)),
        (hxs.at[1], hxr.at[1], device(lax.rem(p + NX - 1, NX), z)),
        (hys.at[0], hyr.at[0], device(p, lax.rem(z + 1, NZ))),
        (hys.at[1], hyr.at[1], device(p, lax.rem(z + NZ - 1, NZ))),
    ]
    for at, (src, dst, target) in enumerate(halos):
        pltpu.make_async_remote_copy(
            src, dst, send_sem.at[3 * CHUNKS + at], h_sem.at[at], device_id=target, device_id_type=MESH
        ).start()
    spread(1)

    def to_z(n):
        wait_all(r[n], a_sem.at[n])

        def part_slots(t, _):
            for s in range(2):
                rd[n][t * 2 + s] = r[n][pl.ds(pl.multiple_of(t * 16, 16) + s, 8, stride=2), :]
            return 0

        lax.fori_loop(0, NX, part_slots, 0, unroll=4)

        if spill:
            for o in range(spill):
                share = rd[n][spill_tab[0, o]]
                for t in range(NZ):
                    v1s[n][t * spill + o] = share[t : t + 1]
            start_z(
                lambda t: v1s[n].at[pl.ds(t * spill, spill)],
                lambda: v1r[n].at[pl.ds(z * spill, spill)],
                v1_sem.at[n],
                send_sem.at[3 * CHUNKS + 6 + n],
            )
        for d in range(NZ - 1, -1, -1):
            to = lax.rem(z + d, NZ)
            span = pl.ds(starts[d], sizes[d])

            def one(q, _):
                zs[n][starts[d] + q] = rd[n][send_tab[0, to * PLACES + q]]
                return 0

            lax.fori_loop(0, sizes[d], one, 0, unroll=sizes[d] if sizes[d] <= 16 else 4)
            if d:
                pltpu.make_async_remote_copy(
                    zs[n].at[span],
                    zr[n].at[span],
                    send_sem.at[CHUNKS + n],
                    z_sem.at[n],
                    device_id=device(p, to),
                    device_id_type=MESH,
                ).start()
            else:
                pltpu.make_async_copy(zs[n].at[span], zr[n].at[span], z_sem.at[n]).start()

    def relay(n):
        if not spill:
            return
        wait_all(v1r[n], v1_sem.at[n])

        def one(e, _):
            v2s[n][e] = v1r[n][relay_tab[0, e // spill * SPILL + lax.rem(e, spill)]]
            return 0

        lax.fori_loop(0, NZ * spill, one, 0, unroll=4)
        start_z(
            lambda t: v2s[n].at[pl.ds(t * spill, spill)],
            lambda: v2r[n].at[pl.ds(z * spill, spill)],
            v2_sem.at[n],
            send_sem.at[4 * CHUNKS + 6 + n],
        )

    def to_owner(n):
        c, half = n // 2, n % 2
        wait_all(zr[n].at[pl.ds(0, total_places)], z_sem.at[n])
        if spill:
            wait_all(v2r[n], v2_sem.at[n])
            for o in range(spill):
                for t in range(NZ):
                    zr[n][total_places + o, t : t + 1, :] = v2r[n][t * spill + o]

        def one(t, _):
            for s in range(2):
                ps[n][t, s] = zr[n][take_tab[0, t * 2 + s]]
            return 0

        lax.fori_loop(0, NX, one, 0, unroll=4)
        start_plane(
            lambda t: ps[n].at[t],
            lambda: boxes_out.at[c, :, pl.ds(pl.multiple_of(half * HALF + p * SHARE, SHARE), SHARE), :],
            p_sem.at[n],
            send_sem.at[2 * CHUNKS + n],
        )

    to_z(0)
    spread(2)
    bt[...] = jnp.zeros_like(bt)
    for c in range(3):
        for k in range(PATCH_Z):
            bt[pl.ds(c * PATCH_Z + k, 32, stride=16), :] = m[c, k + 1, 8:40, :]
    columns = bt[...]
    new_row = new_ref[...]
    local_x = ax_ref[...] - p * 32
    local_y = ay_ref[...] - z * 128
    boxes = new_row.shape[1]
    depth = iota((128, boxes), 0)
    corners = [None] * 4
    for f in range(2):
        hot = jnp.where(depth == local_y + f, 1.0, 0.0)
        picked = jnp.dot(columns, hot, precision=PRECISE, preferred_element_type=F32)
        for e in range(2):
            total = jnp.zeros((16, boxes), F32)
            for x in range(32):
                here = jnp.where(local_x + e == x, 1.0, 0.0)
                total = total + picked[x * 16 : (x + 1) * 16] * here
            corners[e * 2 + f] = total
    terms = jnp.concatenate(corners, axis=0)
    odd = (new_row & 1).astype(F32)
    terms = jnp.concatenate([terms * (1.0 - odd), terms * odd], axis=0)
    owner = jnp.where((new_row >> 1) == iota((boxes, boxes), 0), 1.0, 0.0)
    ts[...] = dot_nt(owner, terms).reshape(NX, NZ, 128)
    start_plane(lambda t: ts.at[t], lambda: tr.at[p], t_sem, send_sem.at[3 * CHUNKS + 4])

    to_z(1)
    relay(0)
    spread(3)
    for at, (_, dst, _) in enumerate(halos):
        wait_all(dst, h_sem.at[at])
    for c in range(3):
        block = slice(c * 64, (c + 1) * 64)
        m[c, 1:65, 7, :] = jnp.where(p > 0, hxr[0, block, :], 0.0)
        m[c, 1:65, 40, :] = jnp.where(p < NX - 1, hxr[1, block, :], 0.0)
    stores = []
    for part in range(4):
        first, last = part * 16, part * 16 + 16
        meso_levels(m, hyr, mout, p, z, first, last)
        span = pl.ds(first, last - first)
        stores.append(pltpu.make_async_copy(mout.at[:, span], meso_out.at[:, span], local_sem.at[part]))
        stores[-1].start()
        to_z(part + 2)
        relay(part + 1)
        if part < 2:
            spread(part + 4)
        if part > 0:
            to_owner(part - 1)

    wait_all(tr, t_sem)
    summed = jnp.sum(tr[...], axis=0)
    for t in range(NZ):
        tz[t] = summed[t : t + 1]
    start_z(lambda t: tz.at[t], lambda: tzr.at[z], tz_sem, send_sem.at[3 * CHUNKS + 5])

    mine = (p * NZ + z) * 2
    hot = jnp.where(new_row == mine + iota((8, boxes), 0), 1.0, 0.0)
    px, py = pxy_ref[:, 0, :], pxy_ref[:, 1, :]
    pz, pc = pz_ref[...], pc_ref[...]
    points_out[...] = dot_nt(hot, jnp.concatenate([px, px, py, py, pz, pz, pc, pc], axis=0))
    fields = jnp.concatenate(
        [
            offset_ref[...].astype(F32),
            shift_ref[...].astype(F32),
            jnp.ones((1, boxes), F32),
            jnp.zeros((123, boxes), F32),
        ],
        axis=0,
    )
    ints_out[...] = jnp.round(dot_nt(hot, fields)).astype(I32)

    relay(CHUNKS - 1)
    for n in range(3, CHUNKS):
        to_owner(n)
    wait_all(tzr, tz_sem)
    patch_out[...] = jnp.sum(tzr[...], axis=0)

    for store in stores:
        store.wait()
    for n in range(CHUNKS):
        wait_all(boxes_out.at[n // 2, :, pl.ds(n % 2 * HALF, HALF), :], p_sem.at[n])

    def sent(ref, sem):
        pltpu.make_async_remote_copy(
            ref, ref, sem, h_sem.at[0], device_id=device(p, z), device_id_type=MESH
        ).wait_send()

    for n in range(CHUNKS):
        sent(r[n].at[pl.ds(0, (NX - 1) * 16), :], send_sem.at[n])
        sent(zs[n].at[pl.ds(sizes[0], total_places - sizes[0])], send_sem.at[CHUNKS + n])
        if spill:
            sent(v1s[n].at[pl.ds(0, (NZ - 1) * spill)], send_sem.at[3 * CHUNKS + 6 + n])
            sent(v2s[n].at[pl.ds(0, (NZ - 1) * spill)], send_sem.at[4 * CHUNKS + 6 + n])
        sent(ps[n].at[pl.ds(0, NX - 1)], send_sem.at[2 * CHUNKS + n])
    for at in range(4):
        sent(halos[at][0], send_sem.at[3 * CHUNKS + at])
    sent(ts.at[pl.ds(0, NX - 1)], send_sem.at[3 * CHUNKS + 4])
    sent(tz.at[pl.ds(0, NZ - 1)], send_sem.at[3 * CHUNKS + 5])


def split_pair(a):
    high = a.astype(jnp.bfloat16)
    return high, (a - high.astype(F32)).astype(jnp.bfloat16)


def gauss_line(distance):
    return jnp.exp(-((distance / KERNEL_WIDTH) ** 2)) / (math.sqrt(math.pi) * KERNEL_WIDTH)


def box_kernel(boxes, meso, patch, points, ints, out, meso_out, held, merged, load_sem, meso_sem):
    loads = []
    for s in range(2):
        for c in range(3):
            loads.append(
                pltpu.make_async_copy(
                    boxes.at[c, s], held.at[s, c, pl.ds(MARGIN, ROWS), :], load_sem.at[s * 3 + c]
                )
            )
            loads[-1].start()
    through = pltpu.make_async_copy(meso, meso_out, meso_sem)
    through.start()
    lane, h = iota((32, 128), 1), iota((32, 128), 0)
    i, j = 2 * h + (lane >> 6), lane & 63
    tall, wide = iota((128, 128), 0), iota((128, 128), 1)
    table = level_table()
    for s in range(2):
        ox, oy, sx, sy, occupied = [ints[s, at] for at in range(5)]
        flat = sx * 64 + sy
        rows, turn = flat >> 7, flat & 127
        valid = (i + sx >= 0) & (i + sx < 64) & (j + sy >= 0) & (j + sy < 64)
        right_x = ((ox + i).astype(F32) + 0.5) / RATIO
        right_y = ((oy + j).astype(F32) + 0.5) / RATIO
        left_x, left_y = 1.0 - right_x, 1.0 - right_y
        weights = [left_x * left_y, left_x * right_y, right_x * left_y, right_x * right_y]
        x_row = points[s : s + 1, 0:128]
        y_row = points[s : s + 1, 128:256]
        z_row = points[s : s + 1, 256:384]
        coef = points[s : s + 1, 384:512]
        kx = gauss_line((2 * iota((32, 128), 0) + (lane >> 6)).astype(F32) + 0.5 - x_row)
        kz = gauss_line(iota((BOX_Z, 128), 0).astype(F32) + 0.5 - z_row)
        ky = gauss_line((tall & 63).astype(F32) + 0.5 - y_row)
        ky = jnp.where((tall >> 6) == (wide >> 6), ky, 0.0)
        ky_high, ky_low = split_pair(ky)
        twice = jnp.concatenate([ky_high, ky_low], axis=1)
        sample_w = jnp.concatenate([twice, twice], axis=0)
        spread_w = jnp.concatenate(
            [jnp.concatenate([ky_high, ky_high], axis=1), jnp.concatenate([ky_low, ky_low], axis=1)], axis=0
        )
        samples = []
        for c in range(3):
            loads[s * 3 + c].wait()
            planes = []
            for k in range(PATCH_Z):
                plane = weights[0] * patch[0, s * 64 + c * PATCH_Z + k]
                for at in range(1, 4):
                    plane = plane + weights[at] * patch[0, s * 64 + at * 16 + c * PATCH_Z + k]
                planes.append(plane)
            for level in range(BOX_Z):
                below, part = table[level]
                fill = planes[below]
                if part:
                    fill = (1.0 - part) * fill + part * planes[below + 1]
                start = MARGIN + level * 32 + rows
                first = held[s, c, pl.ds(start, 32), :]
                second = held[s, c, pl.ds(start + 1, 32), :]
                moved = pltpu.roll(jnp.where(lane >= turn, first, second), 128 - turn, 1)
                merged[s, c, level * 32 : (level + 1) * 32, :] = jnp.where(valid, moved, fill)
            block = merged[s, c]
            high, low = split_pair(block)
            both = jnp.dot(
                jnp.concatenate([high, low], axis=1), sample_w, preferred_element_type=F32
            )
            sums = (both[:, :128] + both[:, 128:]).reshape(BOX_Z, 32, 128) * kx[None]
            per_level = jnp.sum(sums, axis=1) * kz
            half = jnp.sum(per_level, axis=0, keepdims=True)
            samples.append(half + pltpu.roll(half, 64, 1))
        magnitude = jnp.sqrt(1.0 + (samples[0] ** 2 + samples[1] ** 2 + samples[2] ** 2))
        shape = (kz[:, None, :] * kx[None]).reshape(ROWS, 128)
        for c in range(3):
            force = FORCE_GAIN * (-0.5 * coef * magnitude * samples[c])
            high, low = split_pair(shape * force)
            both = lax.dot_general(
                jnp.concatenate([high, low], axis=1),
                spread_w,
                (((1,), (1,)), ((), ())),
                preferred_element_type=F32,
            )
            finished = merged[s, c] + (both[:, :128] + both[:, 128:])
            out[c, pl.ds(s, ROWS, stride=2), :] = jnp.where(occupied > 0, finished, 0.0)
    through.wait()


def vmem():
    return pl.BlockSpec(memory_space=pltpu.VMEM)


def smem():
    return pl.BlockSpec(memory_space=pltpu.SMEM)


def anywhere():
    return pl.BlockSpec(memory_space=pl.ANY)


def exchange(plan, collective_id, operands):
    total_places = places_of(plan[0])[2]
    relays = pltpu.VMEM((NZ * max(plan[1], 1), 1, 128), F32)
    shape = jax.ShapeDtypeStruct
    dma = pltpu.SemaphoreType.DMA
    return pl.pallas_call(
        functools.partial(exchange_kernel, plan),
        out_shape=(
            shape((3, 2, ROWS, 128), F32),
            shape((3, 64, 32, 128), F32),
            shape((1, 128), F32),
            shape((8, 512), F32),
            shape((8, 128), I32),
        ),
        in_specs=[anywhere(), anywhere()] + [smem()] * 4 + [vmem()] * 8,
        out_specs=(anywhere(), anywhere(), vmem(), vmem(), vmem()),
        scratch_shapes=[
            (pltpu.VMEM((ROWS, 128), F32),) * CHUNKS,
            (pltpu.VMEM((2 * NX, SHARE, 128), F32),) * CHUNKS,
            (pltpu.VMEM((total_places, SHARE, 128), F32),) * CHUNKS,
            (pltpu.VMEM((total_places + plan[1], SHARE, 128), F32),) * CHUNKS,
            (relays,) * CHUNKS,
            (relays,) * CHUNKS,
            (relays,) * CHUNKS,
            (relays,) * CHUNKS,
            (pltpu.VMEM((NX, 2, SHARE, 128), F32),) * CHUNKS,
            pltpu.VMEM((3, 66, 48, 128), F32),
            pltpu.VMEM((3, 64, 32, 128), F32),
            pltpu.VMEM((2, 192, 128), F32),
            pltpu.VMEM((2, 192, 128), F32),
            pltpu.VMEM((2, 32, 256), F32),
            pltpu.VMEM((2, 32, 256), F32),
            pltpu.VMEM((512, 128), F32),
            pltpu.VMEM((NX, NZ, 128), F32),
            pltpu.VMEM((NX, NZ, 128), F32),
            pltpu.VMEM((NZ, 1, 128), F32),
            pltpu.VMEM((NZ, 1, 128), F32),
            dma((5 * CHUNKS + 6,)),
            dma((CHUNKS,)),
            dma((CHUNKS,)),
            dma((CHUNKS,)),
            dma((CHUNKS,)),
            dma((CHUNKS,)),
            dma,
            dma,
            dma((4,)),
            dma((5,)),
        ],
        compiler_params=pltpu.CompilerParams(
            collective_id=collective_id, has_side_effects=True, vmem_limit_bytes=56 << 20
        ),
        name="exchange",
    )(*operands)


def local(
    meso_wind,
    old_boxes,
    box_old_slot,
    box_new_slot,
    anchor_x,
    anchor_y,
    box_offset,
    wind_shift,
    point_xy,
    point_z,
    point_coef,
):
    shape = jax.ShapeDtypeStruct
    old_row, new_row = box_old_slot.reshape(1, -1), box_new_slot.reshape(1, -1)
    *routes, choice = pl.pallas_call(
        tables_kernel,
        out_shape=(shape((1, NZ * PLACES), I32),) + (shape((1, 128), I32),) * 4,
        in_specs=[vmem(), vmem()],
        out_specs=(vmem(),) * 5,
        name="tables",
    )(old_row, new_row)
    old = jnp.transpose(old_boxes.reshape(2, 3, ROWS, 128), (1, 2, 0, 3)).reshape(3, 2 * ROWS, 128)
    operands = (
        old,
        meso_wind,
        *routes,
        new_row,
        anchor_x.reshape(1, -1),
        anchor_y.reshape(1, -1),
        box_offset.T,
        wind_shift.T,
        jnp.transpose(point_xy, (1, 2, 0)),
        point_z.T,
        point_coef.T,
    )
    boxes, meso_next, patch, points, ints = lax.switch(
        choice[0, 0],
        [functools.partial(exchange, plan, at + 1) for at, plan in enumerate(PLANS)],
        operands,
    )
    new_boxes, meso_next = pl.pallas_call(
        box_kernel,
        out_shape=(shape((3, 2 * ROWS, 128), F32), shape((3, 64, 32, 128), F32)),
        in_specs=[anywhere(), anywhere(), smem(), vmem(), smem()],
        out_specs=(vmem(), anywhere()),
        scratch_shapes=[
            pltpu.VMEM((2, 3, ROWS + 2 * MARGIN, 128), F32),
            pltpu.VMEM((2, 3, ROWS, 128), F32),
            pltpu.SemaphoreType.DMA((6,)),
            pltpu.SemaphoreType.DMA,
        ],
        compiler_params=pltpu.CompilerParams(vmem_limit_bytes=40 << 20),
        name="boxes",
    )(boxes, meso_next, patch, points, ints)
    new_boxes = jnp.transpose(new_boxes.reshape(3, ROWS, 2, 128), (2, 0, 1, 3)).reshape(2, 3, ROWS * 128)
    return (meso_next, new_boxes)


def solution(mesh):
    whole = P(("grp", "gx", "gy"), None, None)
    grid = P(None, None, ("grp", "gx"), "gy")
    return jax.shard_map(
        local,
        mesh=mesh,
        in_specs=(grid, whole) + (P(),) * 9,
        out_specs=(grid, whole),
        check_vma=False,
    )
```
